32 devices in a mesh: row: 4 (over z), col: 8 (over y, x, core).
Axes of the slice: x: 2, y: 2, z: 4, core: 2. Of those that a mesh axis runs over, the one named last changes fastest.
Arguments:
- modal_velocity: bfloat16 [2048, 128], P('row'), may hold values from -6 to 6
- mode_shapes: bfloat16 [1536, 2048], P('col', 'row'), may hold values from -0.125 to 0.125
- coords: float32 [3, 1536], replicated, may hold values from 0 to 1
- panel_order: int32 [1536], replicated, may hold values from 0 to 1535, each once
- areas: float32 [1536], replicated, may hold values from 0.5 to 2
- weights: float32 [1536], replicated, may hold values from 0.25 to 4
Outputs:
- pressure: float32 [1536, 128], P(('row', 'col'))
- gradient: float32 [2048, 128], P(('row', 'col'))
The draws below stay inside these ranges and needn't reach their ends.
Inputs may be any that keep to these rules, and one draw needn't show every extreme that they name: `panel_order`: each panel index appears exactly once.
All inputs are finite; a program needn't handle non-finite values.
Results may differ from the reference program's by a relative error of at most 0.004.
Values may be sent and summed in bfloat16 or wider, within the bound.
No kernel may reach another device: no remote copies, remote signals or barrier semaphores. Data moves between devices by JAX's collectives and lax.ppermute only.
A program may use at most 64 MiB of HBM per device.

```python
import math
import jax
import jax.numpy as jnp
from jax import lax

PANELS_DEV = 48
MODES = 2048
LOADS = 64
PANELS = 1536


def steps_of(key, extent, shards, least, top_value):
    loudness = 1.0
    for axis_at, blocks in shards:
        heights = jax.random.uniform(jax.random.fold_in(jax.random.fold_in(key, 6), axis_at), (blocks,), jnp.float32, least / len(shards), top_value / len(shards))
        loudness = loudness * jnp.repeat(jnp.exp(heights), extent[axis_at] // blocks).reshape((-1,) + (1,) * (len(extent) - 1 - axis_at))
    return loudness


def scatter_about(key, extent, deviation, limit, split=(), kind=jnp.bfloat16):
    gain = steps_of(key, extent, split, -0.22, 0.18) if split else 1.0
    values = jax.random.normal(key, extent, jnp.float32) * deviation * gain
    return jnp.minimum(jnp.maximum(values, -limit), limit).astype(kind)


def setup_inputs(seed: int = 0) -> dict:
    seeds = jax.random.split(jax.random.key(seed), 7)
    modal_velocity = scatter_about(seeds[0], (MODES, 2 * LOADS), 1.0, 6.0, ((0, 4),))
    mode_shapes = scatter_about(seeds[1], (PANELS, MODES), MODES ** -0.5, 0.125, ((0, 8), (1, 4)))
    coords = jnp.clip(jax.random.uniform(seeds[2], (3, PANELS), jnp.float32, 0.0, 1.0), 0.0, 1.0)
    panel_order = jax.random.permutation(seeds[3], PANELS).astype(jnp.int32)
    areas = jnp.clip(jnp.exp(jax.random.uniform(seeds[4], (PANELS,), jnp.float32, math.log(0.5), math.log(2.0))), 0.5, 2.0)
    weights = jnp.clip(jnp.exp(jax.random.uniform(seeds[5], (PANELS,), jnp.float32, math.log(0.25), math.log(4.0))), 0.25, 4.0)
    return {"modal_velocity": modal_velocity, "mode_shapes": mode_shapes, "coords": coords, "panel_order": panel_order, "areas": areas, "weights": weights}


wavenumber = 20.0
smoothing = 0.02

def green_rows(target, source, source_area, norm_const):
    offset = target[0][:, None] - source[0][None, :]
    square = offset * offset
    offset = target[1][:, None] - source[1][None, :]
    square = square + offset * offset
    offset = target[2][:, None] - source[2][None, :]
    square = square + offset * offset
    distance = jnp.sqrt(square + smoothing * smoothing)
    factor = source_area[None, :] / (distance * norm_const)
    angle_value = wavenumber * distance
    return jnp.stack([factor * jnp.cos(angle_value), factor * jnp.sin(angle_value)]).astype(jnp.bfloat16)

def forward_parts(products, load_count):
    real_part = products[0, :, :load_count] - products[1, :, load_count:]
    imag_part = products[0, :, load_count:] + products[1, :, :load_count]
    return jnp.concatenate([real_part, imag_part], axis=1)

def adjoint_parts(products, load_count):
    real_part = products[0, :, :load_count] + products[1, :, load_count:]
    imag_part = products[0, :, load_count:] - products[1, :, :load_count]
    return jnp.concatenate([real_part, imag_part], axis=1)

def reference(modal_velocity, mode_shapes, coords, panel_order, areas, weights):
    norm_const = math.sqrt(4.0 * math.pi * PANELS)
    placed = jnp.take(coords, panel_order, axis=1)
    area_placed = jnp.take(areas, panel_order)
    weight_placed = jnp.take(weights, panel_order)
    surface = jnp.dot(mode_shapes.astype(jnp.float32), modal_velocity.astype(jnp.float32)).astype(jnp.bfloat16)
    surface_wide = lax.optimization_barrier(surface).astype(jnp.float32)
    block_rows = PANELS_DEV * 8
    block_count = PANELS // block_rows

    def tile_for(block_index):
        first_row = block_index * block_rows
        target = lax.dynamic_slice_in_dim(placed, first_row, block_rows, 1)
        tile = green_rows(target, placed, area_placed, norm_const)
        return lax.optimization_barrier(tile).astype(jnp.float32)

    def forward(block_index):
        products = jnp.einsum('krm,mc->krc', tile_for(block_index), surface_wide)
        return forward_parts(products, LOADS)
    pressure = lax.map(forward, jnp.arange(block_count, dtype=jnp.int32)).reshape(PANELS, 2 * LOADS)
    source = (pressure * weight_placed[:, None]).astype(jnp.bfloat16)
    source_wide = lax.optimization_barrier(source).astype(jnp.float32)

    def adjoint(running, block_index):
        part_rows = lax.dynamic_slice_in_dim(source_wide, block_index * block_rows, block_rows, 0)
        products = jnp.einsum('krm,rc->kmc', tile_for(block_index), part_rows)
        return (running + adjoint_parts(products, LOADS), None)
    sensitivity, _ = lax.scan(adjoint, jnp.zeros((PANELS, 2 * LOADS), jnp.float32), jnp.arange(block_count, dtype=jnp.int32))
    sensitivity = sensitivity.astype(jnp.bfloat16)
    sensitivity_wide = lax.optimization_barrier(sensitivity).astype(jnp.float32)
    gradient = jnp.dot(mode_shapes.astype(jnp.float32).T, sensitivity_wide)
    return (pressure, gradient)
```

```python
import math

import jax
import jax.numpy as jnp
from jax import lax
from jax.sharding import PartitionSpec as P

wavenumber = 20.0
smoothing = 0.02


def green_rows(target, source, source_area, norm_const):
    offset = target[0][:, None] - source[0][None, :]
    square = offset * offset
    offset = target[1][:, None] - source[1][None, :]
    square = square + offset * offset
    offset = target[2][:, None] - source[2][None, :]
    square = square + offset * offset
    distance = jnp.sqrt(square + smoothing * smoothing)
    factor = source_area[None, :] / (distance * norm_const)
    angle_value = wavenumber * distance
    return jnp.stack([factor * jnp.cos(angle_value), factor * jnp.sin(angle_value)]).astype(
        jnp.bfloat16
    )


def make_tile(target, source, source_area, norm_const):
    row_count = target.shape[1]
    if row_count <= 1024 or row_count % 512 != 0:
        return green_rows(target, source, source_area, norm_const)
    buffer = jnp.zeros((2, row_count, source.shape[1]), jnp.bfloat16)

    def fill(block_index, current):
        first_row = block_index * 512
        target_part = lax.dynamic_slice_in_dim(target, first_row, 512, 1)
        return lax.dynamic_update_slice_in_dim(
            current, green_rows(target_part, source, source_area, norm_const), first_row, 1
        )

    return lax.fori_loop(0, row_count // 512, fill, buffer)


def forward_parts(products, load_count):
    real_part = products[0, :, :load_count] - products[1, :, load_count:]
    imag_part = products[0, :, load_count:] + products[1, :, :load_count]
    return jnp.concatenate([real_part, imag_part], axis=1)


def adjoint_parts(products, load_count):
    real_part = products[0, :, :load_count] + products[1, :, load_count:]
    imag_part = products[0, :, load_count:] - products[1, :, :load_count]
    return jnp.concatenate([real_part, imag_part], axis=1)


def row_total(partial_value):
    return lax.psum(partial_value, "row").astype(jnp.bfloat16)


def local_general(modal_velocity, mode_shapes, coords, panel_order, areas, weights):
    row_index = lax.axis_index("row")
    col_index = lax.axis_index("col")
    src_rows = mode_shapes.shape[0]
    panels_each = src_rows // lax.axis_size("row")
    tgt_rows = panels_each * lax.axis_size("col")
    panel_total = panel_order.shape[0]
    norm_const = math.sqrt(4.0 * math.pi * panel_total)
    load_count = modal_velocity.shape[1] // 2
    target_ids = lax.dynamic_slice_in_dim(panel_order, row_index * tgt_rows, tgt_rows)
    source_ids = lax.dynamic_slice_in_dim(panel_order, col_index * src_rows, src_rows)
    target_xyz = jnp.take(coords, target_ids, axis=1)
    source_xyz = jnp.take(coords, source_ids, axis=1)
    source_area = jnp.take(areas, source_ids)
    target_weight = jnp.take(weights, target_ids)
    stored = make_tile(target_xyz, source_xyz, source_area, norm_const)

    def tile_rows():
        return stored

    surface = row_total(jnp.dot(mode_shapes, modal_velocity, preferred_element_type=jnp.float32))
    products = jnp.einsum("krm,mc->krc", tile_rows(), surface, preferred_element_type=jnp.float32)
    pressure = lax.psum_scatter(
        forward_parts(products, load_count), "col", scatter_dimension=0, tiled=True
    )
    own_weight = lax.dynamic_slice_in_dim(target_weight, col_index * panels_each, panels_each)
    source_terms = (pressure * own_weight[:, None]).astype(jnp.bfloat16)
    products = jnp.einsum(
        "krm,rc->kmc",
        tile_rows(),
        lax.all_gather(source_terms, "col", axis=0, tiled=True),
        preferred_element_type=jnp.float32,
    )
    sensitivity = adjoint_parts(products, load_count)
    summed = row_total(sensitivity)
    modal_terms = lax.dot_general(
        mode_shapes, summed, (((0,), (0,)), ((), ())), preferred_element_type=jnp.float32
    )
    gradient = lax.psum_scatter(modal_terms, "col", scatter_dimension=0, tiled=True)
    return (pressure, gradient)


def swap(value, axis, mask):
    return lax.ppermute(value, axis, [(i, i ^ mask) for i in range(lax.axis_size(axis))])


def row_sum(value, wire):
    sent = value.astype(wire)
    parts = [swap(sent, "row", mask) for mask in (1, 2, 3)]
    return value + sum(part.astype(jnp.float32) for part in parts)


def col_sum(value):
    core = lax.axis_index("col") % 2
    half = value.shape[0] // 2
    chip_value = value + swap(value, "col", 1)
    sent = chip_value.astype(jnp.bfloat16)
    near = lax.ppermute(sent, "col", [(i, i ^ (2 if i % 2 == 0 else 4)) for i in range(8)])
    far = swap(lax.dynamic_slice_in_dim(sent, core * half, half), "col", 6)
    zero = jnp.zeros_like(far)
    far = jnp.concatenate([jnp.where(core == 0, far, zero), jnp.where(core == 0, zero, far)], 0)
    others = near.astype(jnp.float32) + far.astype(jnp.float32)
    return chip_value + others + swap(others, "col", 1)


def col_scatter(value):
    col = lax.axis_index("col")
    core, chip = col % 2, col // 2
    blocks = value.reshape(4, 2, value.shape[0] // 8, value.shape[1])
    kept = lax.dynamic_index_in_dim(blocks, core, 1, False)
    kept = kept + swap(lax.dynamic_index_in_dim(blocks, 1 - core, 1, False), "col", 1)
    total = lax.dynamic_index_in_dim(kept, chip, 0, False)
    for mask in (1, 2, 3):
        total = total + swap(lax.dynamic_index_in_dim(kept, chip ^ mask, 0, False), "col", 2 * mask)
    return total


def local(modal_velocity, mode_shapes, coords, panel_order, areas, weights):
    row_index = lax.axis_index("row")
    col_index = lax.axis_index("col")
    src_rows = mode_shapes.shape[0]
    panels_each = src_rows // lax.axis_size("row")
    tgt_rows = panels_each * lax.axis_size("col")
    panel_total = panel_order.shape[0]
    norm_const = math.sqrt(4.0 * math.pi * panel_total)
    load_count = modal_velocity.shape[1] // 2
    target_ids = lax.dynamic_slice_in_dim(panel_order, row_index * tgt_rows, tgt_rows)
    source_ids = lax.dynamic_slice_in_dim(panel_order, col_index * src_rows, src_rows)
    target_xyz = jnp.take(coords, target_ids, axis=1)
    source_xyz = jnp.take(coords, source_ids, axis=1)
    source_area = jnp.take(areas, source_ids)
    target_weight = jnp.take(weights, target_ids)
    tile = green_rows(target_xyz, source_xyz, source_area, norm_const)
    surface = jnp.dot(mode_shapes, modal_velocity, preferred_element_type=jnp.float32)
    surface = row_sum(surface, jnp.bfloat16).astype(jnp.bfloat16)
    products = jnp.einsum("krm,mc->krc", tile, surface, preferred_element_type=jnp.float32)
    pressure = col_sum(forward_parts(products, load_count))
    source_terms = (pressure * target_weight[:, None]).astype(jnp.bfloat16)
    products = jnp.einsum("krm,rc->kmc", tile, source_terms, preferred_element_type=jnp.float32)
    sensitivity = adjoint_parts(products, load_count)
    sensitivity = row_sum(sensitivity, jnp.bfloat16).astype(jnp.bfloat16)
    modal_terms = lax.dot_general(
        mode_shapes, sensitivity, (((0,), (0,)), ((), ())), preferred_element_type=jnp.float32
    )
    own = lax.dynamic_slice_in_dim(pressure, col_index * panels_each, panels_each)
    return (own, col_scatter(modal_terms))


def solution(mesh):
    in_specs = (P("row", None), P("col", "row"), P(), P(), P(), P())
    out_specs = (P(("row", "col"), None), P(("row", "col"), None))
    small = mesh.shape["row"] == 4 and mesh.shape["col"] == 8
    body = local if small else local_general
    return jax.shard_map(body, mesh=mesh, in_specs=in_specs, out_specs=out_specs, check_vma=False)
```

```python
import functools
import math

import jax
import jax.numpy as jnp
from jax import lax
from jax.experimental import pallas as pl
from jax.experimental.pallas import tpu as pltpu
from jax.sharding import PartitionSpec as P

wavenumber = 20.0
smoothing = 0.02


def green_rows(target, source, source_area, norm_const):
    offset = target[0][:, None] - source[0][None, :]
    square = offset * offset
    offset = target[1][:, None] - source[1][None, :]
    square = square + offset * offset
    offset = target[2][:, None] - source[2][None, :]
    square = square + offset * offset
    distance = jnp.sqrt(square + smoothing * smoothing)
    factor = source_area[None, :] / (distance * norm_const)
    angle_value = wavenumber * distance
    return jnp.stack([factor * jnp.cos(angle_value), factor * jnp.sin(angle_value)]).astype(
        jnp.bfloat16
    )


def make_tile(target, source, source_area, norm_const):
    row_count = target.shape[1]
    if row_count <= 1024 or row_count % 512 != 0:
        return green_rows(target, source, source_area, norm_const)
    buffer = jnp.zeros((2, row_count, source.shape[1]), jnp.bfloat16)

    def fill(block_index, current):
        first_row = block_index * 512
        target_part = lax.dynamic_slice_in_dim(target, first_row, 512, 1)
        return lax.dynamic_update_slice_in_dim(
            current, green_rows(target_part, source, source_area, norm_const), first_row, 1
        )

    return lax.fori_loop(0, row_count // 512, fill, buffer)


def forward_parts(products, load_count):
    real_part = products[0, :, :load_count] - products[1, :, load_count:]
    imag_part = products[0, :, load_count:] + products[1, :, :load_count]
    return jnp.concatenate([real_part, imag_part], axis=1)


def adjoint_parts(products, load_count):
    real_part = products[0, :, :load_count] + products[1, :, load_count:]
    imag_part = products[0, :, load_count:] - products[1, :, :load_count]
    return jnp.concatenate([real_part, imag_part], axis=1)


def row_total(partial_value):
    return lax.psum(partial_value, "row").astype(jnp.bfloat16)


def local_general(modal_velocity, mode_shapes, coords, panel_order, areas, weights):
    row_index = lax.axis_index("row")
    col_index = lax.axis_index("col")
    src_rows = mode_shapes.shape[0]
    panels_each = src_rows // lax.axis_size("row")
    tgt_rows = panels_each * lax.axis_size("col")
    panel_total = panel_order.shape[0]
    norm_const = math.sqrt(4.0 * math.pi * panel_total)
    load_count = modal_velocity.shape[1] // 2
    target_ids = lax.dynamic_slice_in_dim(panel_order, row_index * tgt_rows, tgt_rows)
    source_ids = lax.dynamic_slice_in_dim(panel_order, col_index * src_rows, src_rows)
    target_xyz = jnp.take(coords, target_ids, axis=1)
    source_xyz = jnp.take(coords, source_ids, axis=1)
    source_area = jnp.take(areas, source_ids)
    target_weight = jnp.take(weights, target_ids)
    stored = make_tile(target_xyz, source_xyz, source_area, norm_const)

    def tile_rows():
        return stored

    surface = row_total(jnp.dot(mode_shapes, modal_velocity, preferred_element_type=jnp.float32))
    products = jnp.einsum("krm,mc->krc", tile_rows(), surface, preferred_element_type=jnp.float32)
    pressure = lax.psum_scatter(
        forward_parts(products, load_count), "col", scatter_dimension=0, tiled=True
    )
    own_weight = lax.dynamic_slice_in_dim(target_weight, col_index * panels_each, panels_each)
    source_terms = (pressure * own_weight[:, None]).astype(jnp.bfloat16)
    products = jnp.einsum(
        "krm,rc->kmc",
        tile_rows(),
        lax.all_gather(source_terms, "col", axis=0, tiled=True),
        preferred_element_type=jnp.float32,
    )
    sensitivity = adjoint_parts(products, load_count)
    summed = row_total(sensitivity)
    modal_terms = lax.dot_general(
        mode_shapes, summed, (((0,), (0,)), ((), ())), preferred_element_type=jnp.float32
    )
    gradient = lax.psum_scatter(modal_terms, "col", scatter_dimension=0, tiled=True)
    return (pressure, gradient)


sine_terms = (4.442879676818848, -7.307816505432129, 3.5977742671966553, -0.7911993861198425)
cosine_terms = (
    -1.4142135381698608,
    6.978850841522217,
    -5.739460468292236,
    1.883557915687561,
    -0.3106880187988281,
)
lanes = 128
piece = 64
step_rows = 64
whole = pl.BlockSpec(memory_space=pltpu.VMEM)


def call(kernel, outs, scratch, *args, cost=None):
    shapes = tuple(jax.ShapeDtypeStruct(shape, dtype) for shape, dtype in outs)
    return pl.pallas_call(
        kernel,
        out_shape=shapes,
        in_specs=[whole] * len(args),
        out_specs=(whole,) * len(shapes),
        scratch_shapes=[pltpu.VMEM(shape, dtype) for shape, dtype in scratch],
        compiler_params=pltpu.CompilerParams(vmem_limit_bytes=16 * 2**20),
        cost_estimate=cost,
    )(*args)


def horner(terms, value):
    total = jnp.float32(terms[-1])
    for term in terms[-2::-1]:
        total = jnp.float32(term) + value * total
    return total


def place_panels(order_ref, coords_ref, areas_ref, weights_ref, ids, along, down):
    col = lax.axis_index("col")
    chip, core = col // 2, col % 2
    ids[...] = jnp.zeros(ids.shape, jnp.int32)
    count = order_ref.shape[0]
    for at in range(count):
        side, slot, part = at // (count // 2), at % (count // 2) // 3, at % 3
        panel_block = 2 * (chip ^ slot) + (core if side == 0 else 1 - core)
        first = at % 2 * piece
        ids[at // 2 : at // 2 + 1, first : first + piece] = order_ref[pl.ds(3 * panel_block + part, 1), :]
    for group in range(ids.shape[0] // 8):
        index = ids[8 * group : 8 * group + 8, :]
        high, low = index // lanes, index % lanes
        values = [jnp.zeros(index.shape, jnp.float32) for _ in range(5)]
        for part in range(areas_ref.shape[0]):
            chosen = high == part
            rows = [coords_ref[axis : axis + 1, part * lanes : (part + 1) * lanes] for axis in range(3)]
            rows += [areas_ref[part : part + 1, :], weights_ref[part : part + 1, :]]
            for which, row in enumerate(rows):
                found = jnp.take_along_axis(
                    jnp.broadcast_to(row, index.shape), low, axis=1, mode="promise_in_bounds"
                )
                values[which] = jnp.where(chosen, found, values[which])
        for which, value in enumerate(values):
            along[which, 8 * group : 8 * group + 8, :] = value
            down[which, :, 8 * group : 8 * group + 8] = jnp.transpose(value)


def spread_rows(down_ref, rows_ref, first):
    for which in range(4):
        for block in range(rows_ref.shape[1] // lanes):
            at = first + block
            rows_ref[which, block * lanes : (block + 1) * lanes, :] = jnp.broadcast_to(
                down_ref[which, :, at : at + 1], (lanes, lanes)
            )


def fill_green(rows_ref, columns_ref, norm_const, forward_ref, first_row, row_count, adjoint_ref=None):
    def fill(step, carry):
        rows = pl.ds(pl.multiple_of(first_row + step * step_rows, step_rows), step_rows)
        row_x, row_y, row_z, row_area = [rows_ref[which, rows, :] for which in range(4)]
        row_area = row_area * jnp.float32(1.0 / norm_const)
        for part in range(columns_ref.shape[2] // lanes):
            columns = slice(part * lanes, (part + 1) * lanes)
            col_x, col_y, col_z, col_area = [
                jnp.concatenate([columns_ref[which, :, columns]] * (step_rows // 8), 0) for which in range(4)
            ]
            offset_x, offset_y, offset_z = row_x - col_x, row_y - col_y, row_z - col_z
            square = offset_x * offset_x + offset_y * offset_y
            square = square + (offset_z * offset_z + jnp.float32(smoothing * smoothing))
            inverse = lax.rsqrt(square)
            turns = (square * jnp.float32(wavenumber / (2.0 * math.pi))) * inverse
            half_turn = turns - jnp.floor(turns) - jnp.float32(0.5)
            power = half_turn * half_turn
            sine = half_turn * horner(sine_terms, power)
            real_part = sine * sine - jnp.float32(1.0)
            imag_part = sine * horner(cosine_terms, power)
            factor = inverse * col_area
            forward_ref[0, rows, columns] = (real_part * factor).astype(jnp.bfloat16)
            forward_ref[1, rows, columns] = (imag_part * factor).astype(jnp.bfloat16)
            if adjoint_ref is not None:
                factor = inverse * row_area
                adjoint_ref[0, rows, columns] = (real_part * factor).astype(jnp.bfloat16)
                adjoint_ref[1, rows, columns] = (imag_part * factor).astype(jnp.bfloat16)
        return carry

    lax.fori_loop(0, row_count // step_rows, fill, 0)


def first_tile_kernel(
    norm_const,
    order_ref,
    coords_ref,
    areas_ref,
    weights_ref,
    forward_ref,
    adjoint_ref,
    columns_ref,
    down_ref,
    ids,
    along,
    rows_ref,
):
    place_panels(order_ref, coords_ref, areas_ref, weights_ref, ids, along, down_ref)
    for which in range(4):
        scale = jnp.float32(1.0 / norm_const if which == 3 else 1.0)
        for block in range(columns_ref.shape[2] // lanes):
            columns_ref[which, :, block * lanes : (block + 1) * lanes] = jnp.broadcast_to(
                along[which, block : block + 1, :] * scale, (8, lanes)
            )
    spread_rows(down_ref, rows_ref, 0)
    own = adjoint_ref.shape[1]
    fill_green(rows_ref, columns_ref, norm_const, forward_ref, 0, own, adjoint_ref)
    fill_green(rows_ref, columns_ref, norm_const, forward_ref, own, forward_ref.shape[1] - own)


def next_tile_kernel(norm_const, first, columns_ref, down_ref, forward_ref, rows_ref):
    spread_rows(down_ref, rows_ref, first // lanes)
    fill_green(rows_ref, columns_ref, norm_const, forward_ref, 0, forward_ref.shape[1])


def first_tile(coords, panel_order, areas, weights, norm_const, row_count, own_rows):
    panels = panel_order.shape[0]
    blocks = -(-panels // (8 * lanes)) * 8
    wide = (panels // lanes, lanes)
    return call(
        functools.partial(first_tile_kernel, norm_const),
        (
            ((2, row_count, panels), jnp.bfloat16),
            ((2, own_rows, panels), jnp.bfloat16),
            ((4, 8, panels), jnp.float32),
            ((5, lanes, blocks), jnp.float32),
        ),
        (
            ((blocks, lanes), jnp.int32),
            ((5, blocks, lanes), jnp.float32),
            ((4, row_count, lanes), jnp.float32),
        ),
        panel_order.reshape(panels // piece, piece),
        coords,
        areas.reshape(wide),
        weights.reshape(wide),
        cost=pl.CostEstimate(flops=10**9, bytes_accessed=2**22, transcendentals=10**6),
    )


def next_tile(columns, down, norm_const, first, row_count):
    panels = columns.shape[2]
    return call(
        functools.partial(next_tile_kernel, norm_const, first),
        (((2, row_count, panels), jnp.bfloat16),),
        (((4, row_count, lanes), jnp.float32),),
        columns,
        down,
        cost=pl.CostEstimate(flops=10**9, bytes_accessed=2**22, transcendentals=10**6),
    )[0]


def turned(value, sign):
    load_count = value.shape[1] // 2
    first, last = value[:, :load_count], value[:, load_count:]
    if sign > 0:
        return jnp.concatenate([-last, first], 1)
    return jnp.concatenate([last, -first], 1)


def tile_dot(tile_ref, columns, value, sign):
    return jnp.dot(
        tile_ref[0, :, columns], value, preferred_element_type=jnp.float32
    ) + jnp.dot(tile_ref[1, :, columns], turned(value, sign), preferred_element_type=jnp.float32)


def pressure_kernel(side, *refs):
    tile_refs, value_ref, out_ref = refs[:2], refs[2], refs[-1]
    half = value_ref.shape[0]
    columns = slice(side * half, (side + 1) * half)
    first = 0
    for tile_ref in tile_refs:
        rows = slice(first, first + tile_ref.shape[1])
        term = tile_dot(tile_ref, columns, value_ref[...], 1)
        out_ref[rows, :] = term if side == 0 else refs[3][rows, :] + term
        first = rows.stop


def sources(pressure_ref, down_ref, side):
    count = pressure_ref.shape[0] // lanes
    parts = []
    for block in range(count):
        at = side * count + block
        weight = down_ref[4, :, at : at + 1]
        parts.append((pressure_ref[block * lanes : (block + 1) * lanes, :] * weight).astype(jnp.bfloat16))
    return jnp.concatenate(parts, 0)


def own_adjoint_kernel(tile_ref, pressure_ref, down_ref, out_ref):
    half = pressure_ref.shape[0]
    out_ref[...] = tile_dot(tile_ref, slice(0, half), sources(pressure_ref, down_ref, 0), -1)


def modal_kernel(tile_ref, own_ref, other_ref, down_ref, term_ref, modes_ref, modal_ref, pressure_ref):
    row = lax.axis_index("row")
    col = lax.axis_index("col")
    chip, core = col // 2, col % 2
    half = own_ref.shape[0]
    sensitivity = term_ref[...] + tile_dot(
        tile_ref, slice(half, 2 * half), sources(other_ref, down_ref, 1), -1
    )
    modal_ref[...] = lax.dot_general(
        modes_ref[...],
        sensitivity.astype(jnp.bfloat16),
        (((0,), (0,)), ((), ())),
        preferred_element_type=jnp.float32,
    )
    each = pressure_ref.shape[0]
    per_block = modes_ref.shape[0] // each
    panel_block = 2 * row + col // per_block
    first = (panel_block // 2 ^ chip) * modes_ref.shape[0] + col % per_block * each
    rows = pl.ds(pl.multiple_of(first, each), each)
    pressure_ref[...] = jnp.where(panel_block % 2 == core, own_ref[rows, :], other_ref[rows, :])


def swap(value, axis, mask):
    return lax.ppermute(value, axis, [(i, i ^ mask) for i in range(lax.axis_size(axis))])


def col_scatter(value):
    col = lax.axis_index("col")
    core, chip = col % 2, col // 2
    blocks = value.reshape(4, 2, value.shape[0] // 8, value.shape[1])
    kept = lax.dynamic_index_in_dim(blocks, core, 1, False)
    kept = kept + swap(lax.dynamic_index_in_dim(blocks, 1 - core, 1, False), "col", 1)
    total = lax.dynamic_index_in_dim(kept, chip, 0, False)
    for mask in (1, 2, 3):
        total = total + swap(lax.dynamic_index_in_dim(kept, chip ^ mask, 0, False), "col", 2 * mask)
    return total


def local(modal_velocity, mode_shapes, coords, panel_order, areas, weights):
    panels = panel_order.shape[0]
    norm_const = math.sqrt(4.0 * math.pi * panels)
    own_rows, load_columns = mode_shapes.shape[0], modal_velocity.shape[1]
    half = 4 * own_rows
    part_rows = half // 2
    terms = jnp.dot(mode_shapes, modal_velocity, preferred_element_type=jnp.float32)
    sent = terms.astype(jnp.bfloat16)
    received = [swap(sent, "row", mask) for mask in (1, 2, 3)]
    tiles = first_tile(coords, panel_order, areas, weights, norm_const, part_rows, own_rows)
    received, tiles = lax.optimization_barrier((received, tiles))
    tile, own_tile, columns, down = tiles
    surface = (terms + sum(part.astype(jnp.float32) for part in received)).astype(jnp.bfloat16)
    received = [swap(surface, "col", 2 * mask) for mask in (1, 2, 3)]
    last_tile = next_tile(columns, down, norm_const, part_rows, half - part_rows)
    received, last_tile = lax.optimization_barrier((received, last_tile))
    own = jnp.concatenate([surface] + received, 0)
    other = swap(own, "col", 1)
    out = (((half, load_columns), jnp.float32),)
    term = call(functools.partial(pressure_kernel, 0), out, (), tile, last_tile, own)[0]
    pressure = call(functools.partial(pressure_kernel, 1), out, (), tile, last_tile, other, term)[0]
    other = swap(pressure, "col", 1)
    out = (((own_rows, load_columns), jnp.float32),)
    term = call(own_adjoint_kernel, out, (), own_tile, pressure, down)[0]
    modal_terms, own_pressure = call(
        modal_kernel,
        (
            ((mode_shapes.shape[1], load_columns), jnp.float32),
            ((own_rows // lax.axis_size("row"), load_columns), jnp.float32),
        ),
        (),
        own_tile,
        pressure,
        other,
        down,
        term,
        mode_shapes,
    )
    return (own_pressure, col_scatter(modal_terms))


def solution(mesh):
    in_specs = (P("row", None), P("col", "row"), P(), P(), P(), P())
    out_specs = (P(("row", "col"), None), P(("row", "col"), None))

    def body(*args):
        panels = args[3].shape[0]
        small = mesh.shape["row"] == 4 and mesh.shape["col"] == 8 and panels == 1536
        return (local if small else local_general)(*args)

    return jax.shard_map(body, mesh=mesh, in_specs=in_specs, out_specs=out_specs, check_vma=False)
```

```python
import functools
import math

import jax
import jax.numpy as jnp
from jax import lax
from jax.experimental import pallas as pl
from jax.experimental.pallas import tpu as pltpu
from jax.sharding import PartitionSpec as P

wavenumber = 20.0
smoothing = 0.02


def green_rows(target, source, source_area, norm_const):
    offset = target[0][:, None] - source[0][None, :]
    square = offset * offset
    offset = target[1][:, None] - source[1][None, :]
    square = square + offset * offset
    offset = target[2][:, None] - source[2][None, :]
    square = square + offset * offset
    distance = jnp.sqrt(square + smoothing * smoothing)
    factor = source_area[None, :] / (distance * norm_const)
    angle_value = wavenumber * distance
    return jnp.stack([factor * jnp.cos(angle_value), factor * jnp.sin(angle_value)]).astype(
        jnp.bfloat16
    )


def make_tile(target, source, source_area, norm_const):
    row_count = target.shape[1]
    if row_count <= 1024 or row_count % 512 != 0:
        return green_rows(target, source, source_area, norm_const)
    buffer = jnp.zeros((2, row_count, source.shape[1]), jnp.bfloat16)

    def fill(block_index, current):
        first_row = block_index * 512
        target_part = lax.dynamic_slice_in_dim(target, first_row, 512, 1)
        return lax.dynamic_update_slice_in_dim(
            current, green_rows(target_part, source, source_area, norm_const), first_row, 1
        )

    return lax.fori_loop(0, row_count // 512, fill, buffer)


def forward_parts(products, load_count):
    real_part = products[0, :, :load_count] - products[1, :, load_count:]
    imag_part = products[0, :, load_count:] + products[1, :, :load_count]
    return jnp.concatenate([real_part, imag_part], axis=1)


def adjoint_parts(products, load_count):
    real_part = products[0, :, :load_count] + products[1, :, load_count:]
    imag_part = products[0, :, load_count:] - products[1, :, :load_count]
    return jnp.concatenate([real_part, imag_part], axis=1)


def row_total(partial_value):
    return lax.psum(partial_value, "row").astype(jnp.bfloat16)


def local_general(modal_velocity, mode_shapes, coords, panel_order, areas, weights):
    row_index = lax.axis_index("row")
    col_index = lax.axis_index("col")
    src_rows = mode_shapes.shape[0]
    panels_each = src_rows // lax.axis_size("row")
    tgt_rows = panels_each * lax.axis_size("col")
    panel_total = panel_order.shape[0]
    norm_const = math.sqrt(4.0 * math.pi * panel_total)
    load_count = modal_velocity.shape[1] // 2
    target_ids = lax.dynamic_slice_in_dim(panel_order, row_index * tgt_rows, tgt_rows)
    source_ids = lax.dynamic_slice_in_dim(panel_order, col_index * src_rows, src_rows)
    target_xyz = jnp.take(coords, target_ids, axis=1)
    source_xyz = jnp.take(coords, source_ids, axis=1)
    source_area = jnp.take(areas, source_ids)
    target_weight = jnp.take(weights, target_ids)
    stored = make_tile(target_xyz, source_xyz, source_area, norm_const)

    def tile_rows():
        return stored

    surface = row_total(jnp.dot(mode_shapes, modal_velocity, preferred_element_type=jnp.float32))
    products = jnp.einsum("krm,mc->krc", tile_rows(), surface, preferred_element_type=jnp.float32)
    pressure = lax.psum_scatter(
        forward_parts(products, load_count), "col", scatter_dimension=0, tiled=True
    )
    own_weight = lax.dynamic_slice_in_dim(target_weight, col_index * panels_each, panels_each)
    source_terms = (pressure * own_weight[:, None]).astype(jnp.bfloat16)
    products = jnp.einsum(
        "krm,rc->kmc",
        tile_rows(),
        lax.all_gather(source_terms, "col", axis=0, tiled=True),
        preferred_element_type=jnp.float32,
    )
    sensitivity = adjoint_parts(products, load_count)
    summed = row_total(sensitivity)
    modal_terms = lax.dot_general(
        mode_shapes, summed, (((0,), (0,)), ((), ())), preferred_element_type=jnp.float32
    )
    gradient = lax.psum_scatter(modal_terms, "col", scatter_dimension=0, tiled=True)
    return (pressure, gradient)


sine_terms = (4.442879676818848, -7.307816505432129, 3.5977742671966553, -0.7911993861198425)
cosine_terms = (
    -1.4142135381698608,
    6.978850841522217,
    -5.739460468292236,
    1.883557915687561,
    -0.3106880187988281,
)
turn_scale = wavenumber / (2.0 * math.pi)
lanes = 128
step_rows = 64
whole = pl.BlockSpec(memory_space=pltpu.VMEM)
remote = pl.BlockSpec(memory_space=pltpu.HBM)


def call(kernel, outs, scratch, *args, cost=None, specs=None):
    shapes = tuple(jax.ShapeDtypeStruct(shape, dtype) for shape, dtype in outs)
    return pl.pallas_call(
        kernel,
        out_shape=shapes,
        in_specs=specs or [whole] * len(args),
        out_specs=(whole,) * len(shapes),
        scratch_shapes=[entry if not isinstance(entry, tuple) else pltpu.VMEM(*entry) for entry in scratch],
        compiler_params=pltpu.CompilerParams(vmem_limit_bytes=16 * 2**20),
        cost_estimate=cost,
    )(*args)


def horner(terms, value):
    total = jnp.float32(terms[-1])
    for term in terms[-2::-1]:
        total = jnp.float32(term) + value * total
    return total


def place_panels(order_ref, coords_ref, areas_ref, weights_ref, halves, ids, along, down):
    col = lax.axis_index("col")
    chip, core = col // 2, col % 2
    blocks = order_ref.shape[0]
    first_half = lax.broadcasted_iota(jnp.int32, (1, lanes), 1) < lanes // 2
    halves[0, :blocks, :] = order_ref[...]
    halves[1, :blocks, :] = pltpu.roll(order_ref[...], lanes // 2, 1)
    ids[...] = jnp.zeros(ids.shape, jnp.int32)
    for block in range(blocks):
        found = []
        for at in (2 * block, 2 * block + 1):
            side, slot, part = at // blocks, at % blocks // 3, at % 3
            panel_block = 2 * (chip ^ slot) + (core if side == 0 else 1 - core)
            source = 3 * panel_block + part
            found.append(halves[(source + at) % 2, pl.ds(source // 2, 1), :])
        ids[block : block + 1, :] = jnp.where(first_half, found[0], found[1])
    for group in range(ids.shape[0] // 8):
        index = ids[8 * group : 8 * group + 8, :]
        high, low = index // lanes, index % lanes
        values = [jnp.zeros(index.shape, jnp.float32) for _ in range(5)]
        for part in range(areas_ref.shape[0]):
            chosen = high == part
            rows = [coords_ref[axis : axis + 1, part * lanes : (part + 1) * lanes] for axis in range(3)]
            rows += [areas_ref[part : part + 1, :], weights_ref[part : part + 1, :]]
            for which, row in enumerate(rows):
                found = jnp.take_along_axis(
                    jnp.broadcast_to(row, index.shape), low, axis=1, mode="promise_in_bounds"
                )
                values[which] = jnp.where(chosen, found, values[which])
        for which, value in enumerate(values):
            along[which, 8 * group : 8 * group + 8, :] = value
            if which < 3:
                value = value * jnp.float32(turn_scale)
            down[which, :, 8 * group : 8 * group + 8] = jnp.transpose(value)


def spread_rows(down_ref, rows_ref, first):
    for which in range(4):
        for block in range(rows_ref.shape[1] // lanes):
            at = first + block
            rows_ref[which, block * lanes : (block + 1) * lanes, :] = jnp.broadcast_to(
                down_ref[which, :, at : at + 1], (lanes, lanes)
            )


def fill_green(rows_ref, columns_ref, norm_const, forward_ref, adjoint_ref):
    def fill(step, carry):
        rows = pl.ds(pl.multiple_of(step * step_rows, step_rows), step_rows)
        row_x, row_y, row_z, row_area = [rows_ref[which, rows, :] for which in range(4)]
        row_area = row_area * jnp.float32(turn_scale / norm_const)
        for part in range(columns_ref.shape[2] // lanes):
            columns = slice(part * lanes, (part + 1) * lanes)
            col_x, col_y, col_z, col_area = [
                jnp.concatenate([columns_ref[which, :, columns]] * (step_rows // 8), 0) for which in range(4)
            ]
            offset_x, offset_y, offset_z = row_x - col_x, row_y - col_y, row_z - col_z
            square = offset_x * offset_x + offset_y * offset_y
            square = square + (offset_z * offset_z + jnp.float32((smoothing * turn_scale) ** 2))
            inverse = lax.rsqrt(square)
            turns = square * inverse
            half_turn = turns - jnp.floor(turns) - jnp.float32(0.5)
            power = half_turn * half_turn
            sine = half_turn * horner(sine_terms, power)
            cosine = horner(cosine_terms, power)
            for out_ref, area in ((forward_ref, col_area), (adjoint_ref, row_area)):
                factor = inverse * area
                scaled = sine * factor
                out_ref[0, rows, columns] = (scaled * sine - factor).astype(jnp.bfloat16)
                out_ref[1, rows, columns] = (scaled * cosine).astype(jnp.bfloat16)
        return carry

    lax.fori_loop(0, forward_ref.shape[1] // step_rows, fill, 0)


def first_tile_kernel(
    norm_const,
    order_ref,
    coords_ref,
    areas_ref,
    weights_ref,
    forward_ref,
    adjoint_ref,
    columns_ref,
    down_ref,
    halves,
    ids,
    along,
    rows_ref,
):
    place_panels(order_ref, coords_ref, areas_ref, weights_ref, halves, ids, along, down_ref)
    for which in range(4):
        scale = jnp.float32(turn_scale / norm_const if which == 3 else turn_scale)
        for block in range(columns_ref.shape[2] // lanes):
            columns_ref[which, :, block * lanes : (block + 1) * lanes] = jnp.broadcast_to(
                along[which, block : block + 1, :] * scale, (8, lanes)
            )
    spread_rows(down_ref, rows_ref, 0)
    fill_green(rows_ref, columns_ref, norm_const, forward_ref, adjoint_ref)


def next_tile_kernel(norm_const, first, columns_ref, down_ref, forward_ref, adjoint_ref, rows_ref):
    spread_rows(down_ref, rows_ref, first // lanes)
    fill_green(rows_ref, columns_ref, norm_const, forward_ref, adjoint_ref)


def tile_cost(row_count, panels):
    pairs = row_count * panels
    return pl.CostEstimate(flops=40 * pairs, bytes_accessed=8 * pairs, transcendentals=3 * pairs)


def first_tile(order, coords, areas, weights, norm_const, row_count):
    blocks = order.shape[0]
    panels = blocks * lanes
    padded = -(-blocks // 8) * 8
    return call(
        functools.partial(first_tile_kernel, norm_const),
        (
            ((2, row_count, panels), jnp.bfloat16),
            ((2, row_count, panels), jnp.bfloat16),
            ((4, 8, panels), jnp.float32),
            ((5, lanes, padded), jnp.float32),
        ),
        (
            ((2, padded, lanes), jnp.int32),
            ((padded, lanes), jnp.int32),
            ((5, padded, lanes), jnp.float32),
            ((4, -(-row_count // lanes) * lanes, lanes), jnp.float32),
        ),
        order,
        coords,
        areas,
        weights,
        cost=tile_cost(row_count, panels),
    )


def next_tile(columns, down, norm_const, first, row_count):
    panels = columns.shape[2]
    return call(
        functools.partial(next_tile_kernel, norm_const, first),
        (((2, row_count, panels), jnp.bfloat16),) * 2,
        (((4, row_count, lanes), jnp.float32),),
        columns,
        down,
        cost=tile_cost(row_count, panels),
    )


def load_kernel(*refs):
    count = 6
    sources, kept = refs[:count], refs[count : 2 * count - 1]
    terms_ref, sent_ref, velocity, sems = refs[2 * count - 1 :]
    copies = [
        pltpu.make_async_copy(source, target, sems.at[at])
        for at, (source, target) in enumerate(zip(sources, (velocity, *kept)))
    ]
    for copy in copies:
        copy.start()
    copies[0].wait()
    copies[1].wait()
    terms = jnp.dot(kept[0][...], velocity[...], preferred_element_type=jnp.float32)
    terms_ref[...] = terms
    sent_ref[...] = terms.astype(jnp.bfloat16)
    for copy in copies[2:]:
        copy.wait()


def load(modal_velocity, mode_shapes, *tables):
    out = (mode_shapes.shape[0], modal_velocity.shape[1])
    return call(
        load_kernel,
        tuple((value.shape, value.dtype) for value in (mode_shapes, *tables))
        + ((out, jnp.float32), (out, jnp.bfloat16)),
        ((modal_velocity.shape, modal_velocity.dtype), pltpu.SemaphoreType.DMA((6,))),
        *[pltpu.with_memory_space_constraint(value, pltpu.HBM) for value in (modal_velocity, mode_shapes, *tables)],
        specs=[remote] * 6,
    )


def join_kernel(terms_ref, first_ref, second_ref, third_ref, modes_ref, *out_refs):
    chip = lax.axis_index("col") // 2
    count = terms_ref.shape[0]
    total = terms_ref[...]
    for part in (first_ref, second_ref, third_ref):
        total = total + part[...].astype(jnp.float32)
    total = total.astype(jnp.bfloat16)
    for slot, out_ref in enumerate(out_refs):
        out_ref[:count, :] = total
        first = pl.multiple_of((chip ^ slot) * lanes, lanes)
        out_ref[count:, :] = modes_ref[:, pl.ds(first, lanes)]


def turned(value, sign):
    load_count = value.shape[1] // 2
    first, last = value[:, :load_count], value[:, load_count:]
    if sign > 0:
        return jnp.concatenate([-last, first], 1)
    return jnp.concatenate([last, -first], 1)


def tile_dot(tile_ref, columns, value, sign):
    return jnp.dot(
        tile_ref[0, :, columns], value, preferred_element_type=jnp.float32
    ) + jnp.dot(tile_ref[1, :, columns], turned(value, sign), preferred_element_type=jnp.float32)


def pressure_kernel(side, *refs):
    tile_refs, value_ref, out_ref = refs[:2], refs[2], refs[-1]
    half = value_ref.shape[0]
    columns = slice(side * half, (side + 1) * half)
    first = 0
    for tile_ref in tile_refs:
        rows = slice(first, first + tile_ref.shape[1])
        term = tile_dot(tile_ref, columns, value_ref[...], 1)
        out_ref[rows, :] = term if side == 0 else refs[3][rows, :] + term
        first = rows.stop


def sources(pressure_ref, down_ref, side):
    count = pressure_ref.shape[0] // lanes
    parts = []
    for block in range(count):
        at = side * count + block
        weight = down_ref[4, :, at : at + 1]
        parts.append((pressure_ref[block * lanes : (block + 1) * lanes, :] * weight).astype(jnp.bfloat16))
    return jnp.concatenate(parts, 0)


def own_adjoint_kernel(first_ref, second_ref, pressure_ref, down_ref, out_ref):
    half = pressure_ref.shape[0]
    value = sources(pressure_ref, down_ref, 0)
    first = 0
    for tile_ref in (first_ref, second_ref):
        rows = slice(first, first + tile_ref.shape[1])
        out_ref[rows, :] = tile_dot(tile_ref, slice(0, half), value, -1)
        first = rows.stop


def modal_kernel(first_ref, second_ref, own_ref, other_ref, down_ref, term_ref, *refs):
    modes_refs, (kept_ref, sent_ref, pressure_ref, sensitivity) = refs[:4], refs[4:]
    row = lax.axis_index("row")
    col = lax.axis_index("col")
    chip, core = col // 2, col % 2
    half = own_ref.shape[0]
    count = half // 4
    value = sources(other_ref, down_ref, 1)
    first = 0
    for tile_ref in (first_ref, second_ref):
        rows = slice(first, first + tile_ref.shape[1])
        term = term_ref[rows, :] + tile_dot(tile_ref, slice(half, 2 * half), value, -1)
        sensitivity[rows, :] = term.astype(jnp.bfloat16)
        first = rows.stop
    modes = jnp.concatenate([modes_ref[count:, :] for modes_ref in modes_refs], 0)
    modal = lax.dot_general(
        modes, sensitivity[...], (((0,), (0,)), ((), ())), preferred_element_type=jnp.float32
    )
    modes_each = kept_ref.shape[0]
    low, high = modal[:modes_each, :], modal[modes_each:, :]
    kept_ref[...] = jnp.where(core == 0, low, high)
    sent_ref[...] = jnp.where(core == 0, high, low)
    each = pressure_ref.shape[0]
    per_block = count // each
    panel_block = 2 * row + col // per_block
    first = (panel_block // 2 ^ chip) * count + col % per_block * each
    rows = pl.ds(pl.multiple_of(first, each), each)
    pressure_ref[...] = jnp.where(panel_block % 2 == core, own_ref[rows, :], other_ref[rows, :])


def swap(value, axis, mask):
    return lax.ppermute(value, axis, [(i, i ^ mask) for i in range(lax.axis_size(axis))])


def local(modal_velocity, mode_shapes, coords, panel_order, areas, weights):
    panels = panel_order.shape[0]
    norm_const = math.sqrt(4.0 * math.pi * panels)
    own_rows, load_columns = mode_shapes.shape[0], modal_velocity.shape[1]
    half = 4 * own_rows
    part_rows = 256 * half // 768
    wide = (panels // lanes, lanes)
    modes, order, coords, areas, weights, terms, sent = load(
        modal_velocity,
        mode_shapes,
        panel_order.reshape(wide),
        coords,
        areas.reshape(wide),
        weights.reshape(wide),
    )
    received = [swap(sent, "row", mask) for mask in (1, 2, 3)]
    tiles = first_tile(order, coords, areas, weights, norm_const, part_rows)
    received, tiles = lax.optimization_barrier((received, tiles))
    tile, own_tile, columns, down = tiles
    joined = call(
        join_kernel, (((2 * own_rows, load_columns), jnp.bfloat16),) * 4, (), terms, *received, modes
    )
    received = [swap(value, "col", 2 * mask) for mask, value in zip((1, 2, 3), joined[1:])]
    tiles = next_tile(columns, down, norm_const, part_rows, half - part_rows)
    received, (last_tile, last_own_tile) = lax.optimization_barrier((received, tiles))
    joined = [joined[0], *received]
    own = jnp.concatenate([value[:own_rows] for value in joined], 0)
    other = swap(own, "col", 1)
    out = (((half, load_columns), jnp.float32),)
    term = call(functools.partial(pressure_kernel, 0), out, (), tile, last_tile, own)[0]
    pressure = call(functools.partial(pressure_kernel, 1), out, (), tile, last_tile, other, term)[0]
    other = swap(pressure, "col", 1)
    term = call(own_adjoint_kernel, out, (), own_tile, last_own_tile, pressure, down)[0]
    modes_each = mode_shapes.shape[1] // 8
    kept, sent, own_pressure = call(
        modal_kernel,
        (
            ((modes_each, load_columns), jnp.float32),
            ((modes_each, load_columns), jnp.float32),
            ((own_rows // lax.axis_size("row"), load_columns), jnp.float32),
        ),
        (((half, load_columns), jnp.bfloat16),),
        own_tile,
        last_own_tile,
        pressure,
        other,
        down,
        term,
        *joined,
    )
    return (own_pressure, kept + swap(sent, "col", 1))


def solution(mesh):
    in_specs = (P("row", None), P("col", "row"), P(), P(), P(), P())
    out_specs = (P(("row", "col"), None), P(("row", "col"), None))

    def body(*args):
        panels = args[3].shape[0]
        small = mesh.shape["row"] == 4 and mesh.shape["col"] == 8 and panels == 1536
        return (local if small else local_general)(*args)

    return jax.shard_map(body, mesh=mesh, in_specs=in_specs, out_specs=out_specs, check_vma=False)
```

```python
import functools
import math

import jax
import jax.numpy as jnp
from jax import lax
from jax.experimental import pallas as pl
from jax.experimental.pallas import tpu as pltpu
from jax.sharding import PartitionSpec as P

wavenumber = 20.0
smoothing = 0.02


def green_rows(target, source, source_area, norm_const):
    offset = target[0][:, None] - source[0][None, :]
    square = offset * offset
    offset = target[1][:, None] - source[1][None, :]
    square = square + offset * offset
    offset = target[2][:, None] - source[2][None, :]
    square = square + offset * offset
    distance = jnp.sqrt(square + smoothing * smoothing)
    factor = source_area[None, :] / (distance * norm_const)
    angle_value = wavenumber * distance
    return jnp.stack([factor * jnp.cos(angle_value), factor * jnp.sin(angle_value)]).astype(
        jnp.bfloat16
    )


def make_tile(target, source, source_area, norm_const):
    row_count = target.shape[1]
    if row_count <= 1024 or row_count % 512 != 0:
        return green_rows(target, source, source_area, norm_const)
    buffer = jnp.zeros((2, row_count, source.shape[1]), jnp.bfloat16)

    def fill(block_index, current):
        first_row = block_index * 512
        target_part = lax.dynamic_slice_in_dim(target, first_row, 512, 1)
        return lax.dynamic_update_slice_in_dim(
            current, green_rows(target_part, source, source_area, norm_const), first_row, 1
        )

    return lax.fori_loop(0, row_count // 512, fill, buffer)


def forward_parts(products, load_count):
    real_part = products[0, :, :load_count] - products[1, :, load_count:]
    imag_part = products[0, :, load_count:] + products[1, :, :load_count]
    return jnp.concatenate([real_part, imag_part], axis=1)


def adjoint_parts(products, load_count):
    real_part = products[0, :, :load_count] + products[1, :, load_count:]
    imag_part = products[0, :, load_count:] - products[1, :, :load_count]
    return jnp.concatenate([real_part, imag_part], axis=1)


def row_total(partial_value):
    return lax.psum(partial_value, "row").astype(jnp.bfloat16)


def local_general(modal_velocity, mode_shapes, coords, panel_order, areas, weights):
    row_index = lax.axis_index("row")
    col_index = lax.axis_index("col")
    src_rows = mode_shapes.shape[0]
    panels_each = src_rows // lax.axis_size("row")
    tgt_rows = panels_each * lax.axis_size("col")
    panel_total = panel_order.shape[0]
    norm_const = math.sqrt(4.0 * math.pi * panel_total)
    load_count = modal_velocity.shape[1] // 2
    target_ids = lax.dynamic_slice_in_dim(panel_order, row_index * tgt_rows, tgt_rows)
    source_ids = lax.dynamic_slice_in_dim(panel_order, col_index * src_rows, src_rows)
    target_xyz = jnp.take(coords, target_ids, axis=1)
    source_xyz = jnp.take(coords, source_ids, axis=1)
    source_area = jnp.take(areas, source_ids)
    target_weight = jnp.take(weights, target_ids)
    stored = make_tile(target_xyz, source_xyz, source_area, norm_const)

    def tile_rows():
        return stored

    surface = row_total(jnp.dot(mode_shapes, modal_velocity, preferred_element_type=jnp.float32))
    products = jnp.einsum("krm,mc->krc", tile_rows(), surface, preferred_element_type=jnp.float32)
    pressure = lax.psum_scatter(
        forward_parts(products, load_count), "col", scatter_dimension=0, tiled=True
    )
    own_weight = lax.dynamic_slice_in_dim(target_weight, col_index * panels_each, panels_each)
    source_terms = (pressure * own_weight[:, None]).astype(jnp.bfloat16)
    products = jnp.einsum(
        "krm,rc->kmc",
        tile_rows(),
        lax.all_gather(source_terms, "col", axis=0, tiled=True),
        preferred_element_type=jnp.float32,
    )
    sensitivity = adjoint_parts(products, load_count)
    summed = row_total(sensitivity)
    modal_terms = lax.dot_general(
        mode_shapes, summed, (((0,), (0,)), ((), ())), preferred_element_type=jnp.float32
    )
    gradient = lax.psum_scatter(modal_terms, "col", scatter_dimension=0, tiled=True)
    return (pressure, gradient)


sine_terms = (4.442879676818848, -7.307816505432129, 3.5977742671966553, -0.7911993861198425)
cosine_terms = (1.4142040014266968, -6.97763729095459, 5.715188026428223, -1.728213906288147)
turn_scale = wavenumber / (2.0 * math.pi)
lanes = 128
step_rows = 64
whole = pl.BlockSpec(memory_space=pltpu.VMEM)
remote = pl.BlockSpec(memory_space=pltpu.HBM)


def call(kernel, shapes, scratch, *args, cost=None, specs=None, outs=None):
    shapes = tuple(jax.ShapeDtypeStruct(shape, dtype) for shape, dtype in shapes)
    return pl.pallas_call(
        kernel,
        out_shape=shapes,
        in_specs=specs or [whole] * len(args),
        out_specs=outs or (whole,) * len(shapes),
        scratch_shapes=[pltpu.VMEM(*entry) if isinstance(entry, tuple) else entry for entry in scratch],
        compiler_params=pltpu.CompilerParams(vmem_limit_bytes=16 * 2**20),
        cost_estimate=cost,
    )(*args)


def horner(terms, value):
    total = jnp.float32(terms[-1])
    for term in terms[-2::-1]:
        total = jnp.float32(term) + value * total
    return total


def found_at(row_of, index, count):
    high, low = index // lanes, index % lanes
    total = None
    for part in range(count):
        row = row_of(part)
        found = jnp.take_along_axis(
            jnp.broadcast_to(row, index.shape), low, axis=1, mode="promise_in_bounds"
        )
        total = jnp.where(high == part, found, jnp.zeros_like(found) if total is None else total)
    return total


def place_panels(order_ref, coords_ref, areas_ref, weights_ref, halves, ids, along, down):
    col = lax.axis_index("col")
    chip, core = col // 2, col % 2
    blocks = order_ref.shape[0]
    first_half = lax.broadcasted_iota(jnp.int32, (1, lanes), 1) < lanes // 2
    halves[0, :blocks, :] = order_ref[...]
    halves[1, :blocks, :] = pltpu.roll(order_ref[...], lanes // 2, 1)
    ids[...] = jnp.zeros(ids.shape, jnp.int32)
    for block in range(blocks):
        found = []
        for at in (2 * block, 2 * block + 1):
            side, slot, part = at // blocks, at % blocks // 3, at % 3
            panel_block = 2 * (chip ^ slot) + (core if side == 0 else 1 - core)
            source = 3 * panel_block + part
            found.append(halves[(source + at) % 2, pl.ds(source // 2, 1), :])
        ids[block : block + 1, :] = jnp.where(first_half, found[0], found[1])

    def table(which):
        if which < 3:
            return lambda part: coords_ref[which : which + 1, part * lanes : (part + 1) * lanes]
        source = areas_ref if which == 3 else weights_ref
        return lambda part: source[part : part + 1, :]

    for group in range(ids.shape[0] // 8):
        rows = slice(8 * group, 8 * group + 8)
        for which in range(4):
            along[which, rows, :] = found_at(table(which), ids[rows, :], blocks)
    shape = (8, lanes)
    place = lax.broadcasted_iota(jnp.int32, shape, 0) * lanes + lax.broadcasted_iota(jnp.int32, shape, 1)
    each = blocks * lanes // 32
    block = ((place.astype(jnp.float32) + jnp.float32(0.5)) * jnp.float32(1.0 / each)).astype(jnp.int32)
    index = found_at(lambda part: order_ref[part : part + 1, :], place + each * (block + core), blocks)
    for at, which in enumerate((0, 1, 2, 4)):
        value = found_at(table(which), index, blocks)
        down[at] = jnp.transpose(value * jnp.float32(turn_scale) if which < 3 else value)


def spread_rows(down_ref, rows_ref, first):
    for which in range(3):
        for block in range(rows_ref.shape[1] // lanes):
            at = first + block
            rows_ref[which, block * lanes : (block + 1) * lanes, :] = jnp.broadcast_to(
                down_ref[which, :, at : at + 1], (lanes, lanes)
            )


def fill_green(rows_ref, columns_ref, tile_ref):
    def fill(step, carry):
        rows = pl.ds(pl.multiple_of(step * step_rows, step_rows), step_rows)
        row_x, row_y, row_z = [rows_ref[which, rows, :] for which in range(3)]
        for part in range(columns_ref.shape[2] // lanes):
            columns = slice(part * lanes, (part + 1) * lanes)
            col_x, col_y, col_z, col_area = [
                jnp.concatenate([columns_ref[which, :, columns]] * (step_rows // 8), 0) for which in range(4)
            ]
            offset_x, offset_y, offset_z = row_x - col_x, row_y - col_y, row_z - col_z
            square = offset_x * offset_x + offset_y * offset_y
            square = square + (offset_z * offset_z + jnp.float32((smoothing * turn_scale) ** 2))
            inverse = lax.rsqrt(square)
            turns = square * inverse
            half_turn = turns - jnp.round(turns)
            power = half_turn * half_turn
            sine = half_turn * horner(sine_terms, power)
            factor = inverse * col_area
            scaled = sine * factor
            tile_ref[0, rows, columns] = (factor - scaled * sine).astype(jnp.bfloat16)
            tile_ref[1, rows, columns] = (scaled * horner(cosine_terms, power)).astype(jnp.bfloat16)
        return carry

    lax.fori_loop(0, tile_ref.shape[1] // step_rows, fill, 0)


def first_tile_kernel(
    norm_const,
    order_ref,
    coords_ref,
    areas_ref,
    weights_ref,
    tile_ref,
    columns_ref,
    down_ref,
    halves,
    ids,
    along,
    rows_ref,
):
    place_panels(order_ref, coords_ref, areas_ref, weights_ref, halves, ids, along, down_ref)
    for which in range(4):
        scale = jnp.float32(turn_scale / norm_const if which == 3 else turn_scale)
        for block in range(columns_ref.shape[2] // lanes):
            columns_ref[which, :, block * lanes : (block + 1) * lanes] = jnp.broadcast_to(
                along[which, block : block + 1, :] * scale, (8, lanes)
            )
    spread_rows(down_ref, rows_ref, 0)
    fill_green(rows_ref, columns_ref, tile_ref)


def next_tile_kernel(first, columns_ref, down_ref, tile_ref, rows_ref):
    spread_rows(down_ref, rows_ref, first // lanes)
    fill_green(rows_ref, columns_ref, tile_ref)


def tile_cost(row_count, panels):
    pairs = row_count * panels
    return pl.CostEstimate(flops=40 * pairs, bytes_accessed=4 * pairs, transcendentals=3 * pairs)


def first_tile(order, coords, areas, weights, norm_const, row_count):
    blocks = order.shape[0]
    panels = blocks * lanes
    padded = -(-blocks // 8) * 8
    return call(
        functools.partial(first_tile_kernel, norm_const),
        (
            ((2, row_count, panels), jnp.bfloat16),
            ((4, 8, panels), jnp.float32),
            ((4, lanes, 8), jnp.float32),
        ),
        (
            ((2, padded, lanes), jnp.int32),
            ((padded, lanes), jnp.int32),
            ((4, padded, lanes), jnp.float32),
            ((3, row_count, lanes), jnp.float32),
        ),
        order,
        coords,
        areas,
        weights,
        cost=tile_cost(row_count, panels),
    )


def next_tile(columns, down, first, row_count):
    panels = columns.shape[2]
    return call(
        functools.partial(next_tile_kernel, first),
        (((2, row_count, panels), jnp.bfloat16),),
        (((3, row_count, lanes), jnp.float32),),
        columns,
        down,
        cost=tile_cost(row_count, panels),
    )[0]


def load_kernel(*refs):
    count = 6
    sources, kept = refs[:count], refs[count : 2 * count - 1]
    terms_ref, sent_ref, velocity, sems = refs[2 * count - 1 :]
    copies = [
        pltpu.make_async_copy(source, target, sems.at[at])
        for at, (source, target) in enumerate(zip(sources, (velocity, *kept)))
    ]
    for copy in copies:
        copy.start()
    copies[0].wait()
    copies[1].wait()
    terms = jnp.dot(kept[0][...], velocity[...], preferred_element_type=jnp.float32)
    terms_ref[...] = terms
    sent_ref[...] = terms.astype(jnp.bfloat16)
    for copy in copies[2:]:
        copy.wait()


def load(modal_velocity, mode_shapes, *tables):
    out = (mode_shapes.shape[0], modal_velocity.shape[1])
    return call(
        load_kernel,
        tuple((value.shape, value.dtype) for value in (mode_shapes, *tables))
        + ((out, jnp.float32), (out, jnp.bfloat16)),
        ((modal_velocity.shape, modal_velocity.dtype), pltpu.SemaphoreType.DMA((6,))),
        *[pltpu.with_memory_space_constraint(value, pltpu.HBM) for value in (modal_velocity, mode_shapes, *tables)],
        specs=[remote] * 6,
    )


def join_kernel(terms_ref, first_ref, second_ref, third_ref, modes_ref, *out_refs):
    chip = lax.axis_index("col") // 2
    count = terms_ref.shape[0]
    total = terms_ref[...]
    for part in (first_ref, second_ref, third_ref):
        total = total + part[...].astype(jnp.float32)
    total = total.astype(jnp.bfloat16)
    for slot, out_ref in enumerate(out_refs):
        out_ref[:count, :] = total
        first = pl.multiple_of((chip ^ slot) * lanes, lanes)
        out_ref[count:, :] = modes_ref[:, pl.ds(first, lanes)]


def turned(value, sign):
    load_count = value.shape[1] // 2
    first, last = value[:, :load_count], value[:, load_count:]
    if sign > 0:
        return jnp.concatenate([-last, first], 1)
    return jnp.concatenate([last, -first], 1)


def tile_dot(tile_ref, columns, value, sign):
    return jnp.dot(
        tile_ref[0, :, columns], value, preferred_element_type=jnp.float32
    ) + jnp.dot(tile_ref[1, :, columns], turned(value, sign), preferred_element_type=jnp.float32)


def tiles_dot(tile_refs, columns, value, sign, store):
    first = 0
    for tile_ref in tile_refs:
        rows = slice(first, first + tile_ref.shape[1])
        store(rows, tile_dot(tile_ref, columns, value, sign))
        first = rows.stop


def own_pressure_kernel(first_ref, second_ref, value_ref, down_ref, out_ref, weight_ref):
    half = value_ref.shape[0]

    def store(rows, term):
        out_ref[rows, :] = term

    tiles_dot((first_ref, second_ref), slice(0, half), value_ref[...], 1, store)
    for block in range(weight_ref.shape[0] // lanes):
        weight_ref[block * lanes : (block + 1) * lanes, :] = jnp.broadcast_to(
            down_ref[3, :, block : block + 1], (lanes, lanes)
        )


def other_pressure_kernel(first_ref, second_ref, value_ref, term_ref, out_ref):
    half = value_ref.shape[0]

    def store(rows, term):
        out_ref[rows, :] = term_ref[rows, :] + term

    tiles_dot((first_ref, second_ref), slice(half, 2 * half), value_ref[...], 1, store)


def modal_kernel(first_ref, second_ref, value_ref, weight_ref, own_ref, other_ref, *refs):
    kept_ref, sent_ref, pressure_ref, sem = refs
    col = lax.axis_index("col")
    each = pressure_ref.shape[0]
    block = (lax.axis_index("row") * lax.axis_size("col") + col) // 2
    rows = pl.ds(pl.multiple_of(block * each, each), each)
    copy = pltpu.make_async_copy(value_ref.at[rows, :], pressure_ref, sem)
    copy.start()
    source = (value_ref[...] * weight_ref[...]).astype(jnp.bfloat16)
    across, turned_across = jnp.transpose(source), jnp.transpose(turned(source, -1))
    sensitivity = None
    first = 0
    for tile_ref in (first_ref, second_ref):
        targets = slice(first, first + tile_ref.shape[1])
        first = targets.stop
        for part, value in enumerate((across, turned_across)):
            term = jnp.dot(value[:, targets], tile_ref[part], preferred_element_type=jnp.float32)
            sensitivity = term if sensitivity is None else sensitivity + term
    sensitivity = sensitivity.astype(jnp.bfloat16)
    half = own_ref.shape[0]
    modal = jnp.dot(sensitivity[:, :half], own_ref[...], preferred_element_type=jnp.float32)
    modal = modal + jnp.dot(sensitivity[:, half:], other_ref[...], preferred_element_type=jnp.float32)
    modal = jnp.transpose(modal)
    modes_each = kept_ref.shape[0]
    low, high = modal[:modes_each, :], modal[modes_each:, :]
    kept_ref[...] = jnp.where(col % 2 == 0, low, high)
    sent_ref[...] = jnp.where(col % 2 == 0, high, low)
    copy.wait()


def swap(value, axis, mask):
    return lax.ppermute(value, axis, [(i, i ^ mask) for i in range(lax.axis_size(axis))])


def local(modal_velocity, mode_shapes, coords, panel_order, areas, weights):
    panels = panel_order.shape[0]
    norm_const = math.sqrt(4.0 * math.pi * panels)
    own_rows, load_columns = mode_shapes.shape[0], modal_velocity.shape[1]
    half = 4 * own_rows
    part_rows = 256 * half // 768
    wide = (panels // lanes, lanes)
    modes, order, coords, areas, weights, terms, sent = load(
        modal_velocity,
        mode_shapes,
        panel_order.reshape(wide),
        coords,
        areas.reshape(wide),
        weights.reshape(wide),
    )
    received = [swap(sent, "row", mask) for mask in (3, 2, 1)]
    tiles = first_tile(order, coords, areas, weights, norm_const, part_rows)
    received, tiles = lax.optimization_barrier((received, tiles))
    tile, columns, down = tiles
    joined = call(
        join_kernel, (((2 * own_rows, load_columns), jnp.bfloat16),) * 4, (), terms, *received, modes
    )
    received = [swap(value, "col", 2 * mask) for mask, value in zip((1, 2, 3), joined[1:])]
    last_tile = next_tile(columns, down, part_rows, half - part_rows)
    received, last_tile = lax.optimization_barrier((received, last_tile))
    joined = [joined[0], *received]
    own = jnp.concatenate([value[:own_rows] for value in joined], 0)
    other = swap(own, "col", 1)
    out = ((half, load_columns), jnp.float32)
    term, weight = call(
        own_pressure_kernel, (out, ((half, lanes), jnp.float32)), (), tile, last_tile, own, down
    )
    modes = jnp.concatenate([value[own_rows:] for value in joined], 0)
    modes, term = lax.optimization_barrier((modes, term))
    other_modes = swap(modes, "col", 1)
    pressure = call(other_pressure_kernel, (out,), (), tile, last_tile, other, term)[0]
    modes_each = mode_shapes.shape[1] // 8
    kept, sent, own_pressure = call(
        modal_kernel,
        (
            ((modes_each, load_columns), jnp.float32),
            ((modes_each, load_columns), jnp.float32),
            ((own_rows // lax.axis_size("row"), load_columns), jnp.float32),
        ),
        (pltpu.SemaphoreType.DMA,),
        tile,
        last_tile,
        pressure,
        weight,
        modes,
        other_modes,
        outs=(whole, whole, remote),
    )
    return (own_pressure, kept + swap(sent, "col", 1))


def solution(mesh):
    in_specs = (P("row", None), P("col", "row"), P(), P(), P(), P())
    out_specs = (P(("row", "col"), None), P(("row", "col"), None))

    def body(*args):
        panels = args[3].shape[0]
        small = mesh.shape["row"] == 4 and mesh.shape["col"] == 8 and panels == 1536
        return (local if small else local_general)(*args)

    return jax.shard_map(body, mesh=mesh, in_specs=in_specs, out_specs=out_specs, check_vma=False)
```

```python
import functools
import math

import jax
import jax.numpy as jnp
from jax import lax
from jax.experimental import pallas as pl
from jax.experimental.pallas import tpu as pltpu
from jax.sharding import PartitionSpec as P

wavenumber = 20.0
smoothing = 0.02


def green_rows(target, source, source_area, norm_const):
    offset = target[0][:, None] - source[0][None, :]
    square = offset * offset
    offset = target[1][:, None] - source[1][None, :]
    square = square + offset * offset
    offset = target[2][:, None] - source[2][None, :]
    square = square + offset * offset
    distance = jnp.sqrt(square + smoothing * smoothing)
    factor = source_area[None, :] / (distance * norm_const)
    angle_value = wavenumber * distance
    return jnp.stack([factor * jnp.cos(angle_value), factor * jnp.sin(angle_value)]).astype(
        jnp.bfloat16
    )


def make_tile(target, source, source_area, norm_const):
    row_count = target.shape[1]
    if row_count <= 1024 or row_count % 512 != 0:
        return green_rows(target, source, source_area, norm_const)
    buffer = jnp.zeros((2, row_count, source.shape[1]), jnp.bfloat16)

    def fill(block_index, current):
        first_row = block_index * 512
        target_part = lax.dynamic_slice_in_dim(target, first_row, 512, 1)
        return lax.dynamic_update_slice_in_dim(
            current, green_rows(target_part, source, source_area, norm_const), first_row, 1
        )

    return lax.fori_loop(0, row_count // 512, fill, buffer)


def forward_parts(products, load_count):
    real_part = products[0, :, :load_count] - products[1, :, load_count:]
    imag_part = products[0, :, load_count:] + products[1, :, :load_count]
    return jnp.concatenate([real_part, imag_part], axis=1)


def adjoint_parts(products, load_count):
    real_part = products[0, :, :load_count] + products[1, :, load_count:]
    imag_part = products[0, :, load_count:] - products[1, :, :load_count]
    return jnp.concatenate([real_part, imag_part], axis=1)


def row_total(partial_value):
    return lax.psum(partial_value, "row").astype(jnp.bfloat16)


def local_general(modal_velocity, mode_shapes, coords, panel_order, areas, weights):
    row_index = lax.axis_index("row")
    col_index = lax.axis_index("col")
    src_rows = mode_shapes.shape[0]
    panels_each = src_rows // lax.axis_size("row")
    tgt_rows = panels_each * lax.axis_size("col")
    panel_total = panel_order.shape[0]
    norm_const = math.sqrt(4.0 * math.pi * panel_total)
    load_count = modal_velocity.shape[1] // 2
    target_ids = lax.dynamic_slice_in_dim(panel_order, row_index * tgt_rows, tgt_rows)
    source_ids = lax.dynamic_slice_in_dim(panel_order, col_index * src_rows, src_rows)
    target_xyz = jnp.take(coords, target_ids, axis=1)
    source_xyz = jnp.take(coords, source_ids, axis=1)
    source_area = jnp.take(areas, source_ids)
    target_weight = jnp.take(weights, target_ids)
    stored = make_tile(target_xyz, source_xyz, source_area, norm_const)

    def tile_rows():
        return stored

    surface = row_total(jnp.dot(mode_shapes, modal_velocity, preferred_element_type=jnp.float32))
    products = jnp.einsum("krm,mc->krc", tile_rows(), surface, preferred_element_type=jnp.float32)
    pressure = lax.psum_scatter(
        forward_parts(products, load_count), "col", scatter_dimension=0, tiled=True
    )
    own_weight = lax.dynamic_slice_in_dim(target_weight, col_index * panels_each, panels_each)
    source_terms = (pressure * own_weight[:, None]).astype(jnp.bfloat16)
    products = jnp.einsum(
        "krm,rc->kmc",
        tile_rows(),
        lax.all_gather(source_terms, "col", axis=0, tiled=True),
        preferred_element_type=jnp.float32,
    )
    sensitivity = adjoint_parts(products, load_count)
    summed = row_total(sensitivity)
    modal_terms = lax.dot_general(
        mode_shapes, summed, (((0,), (0,)), ((), ())), preferred_element_type=jnp.float32
    )
    gradient = lax.psum_scatter(modal_terms, "col", scatter_dimension=0, tiled=True)
    return (pressure, gradient)


sine_terms = (4.442879676818848, -7.307816505432129, 3.5977742671966553, -0.7911993861198425)
cosine_terms = (1.4142040014266968, -6.97763729095459, 5.715188026428223, -1.728213906288147)
turn_scale = wavenumber / (2.0 * math.pi)
lanes = 128
step_rows = 64
whole = pl.BlockSpec(memory_space=pltpu.VMEM)
remote = pl.BlockSpec(memory_space=pltpu.HBM)


def call(kernel, shapes, scratch, *args, cost=None, specs=None, outs=None, aliases=None):
    shapes = tuple(jax.ShapeDtypeStruct(shape, dtype) for shape, dtype in shapes)
    return pl.pallas_call(
        kernel,
        out_shape=shapes,
        in_specs=specs or [whole] * len(args),
        out_specs=outs or (whole,) * len(shapes),
        scratch_shapes=[pltpu.VMEM(*entry) if isinstance(entry, tuple) else entry for entry in scratch],
        compiler_params=pltpu.CompilerParams(vmem_limit_bytes=16 * 2**20),
        cost_estimate=cost,
        input_output_aliases=aliases or {},
    )(*args)


def horner(terms, value):
    total = jnp.float32(terms[-1])
    for term in terms[-2::-1]:
        total = jnp.float32(term) + value * total
    return total


def found_at(row_of, index, count):
    high, low = index // lanes, index % lanes
    total = None
    for part in range(count):
        row = row_of(part)
        found = jnp.take_along_axis(
            jnp.broadcast_to(row, index.shape), low, axis=1, mode="promise_in_bounds"
        )
        total = jnp.where(high == part, found, jnp.zeros_like(found) if total is None else total)
    return total


def place_panels(order_ref, coords_ref, areas_ref, weights_ref, halves, ids, along, down):
    col = lax.axis_index("col")
    chip, core = col // 2, col % 2
    blocks = order_ref.shape[0]
    first_half = lax.broadcasted_iota(jnp.int32, (1, lanes), 1) < lanes // 2
    halves[0, :blocks, :] = order_ref[...]
    halves[1, :blocks, :] = pltpu.roll(order_ref[...], lanes // 2, 1)
    ids[...] = jnp.zeros(ids.shape, jnp.int32)
    for block in range(blocks):
        found = []
        for at in (2 * block, 2 * block + 1):
            side, slot, part = at // blocks, at % blocks // 3, at % 3
            panel_block = 2 * (chip ^ slot) + (core if side == 0 else 1 - core)
            source = 3 * panel_block + part
            found.append(halves[(source + at) % 2, pl.ds(source // 2, 1), :])
        ids[block : block + 1, :] = jnp.where(first_half, found[0], found[1])

    def table(which):
        if which < 3:
            return lambda part: coords_ref[which : which + 1, part * lanes : (part + 1) * lanes]
        source = areas_ref if which == 3 else weights_ref
        return lambda part: source[part : part + 1, :]

    for group in range(ids.shape[0] // 8):
        rows = slice(8 * group, 8 * group + 8)
        for which in range(4):
            along[which, rows, :] = found_at(table(which), ids[rows, :], blocks)
    shape = (8, lanes)
    place = lax.broadcasted_iota(jnp.int32, shape, 0) * lanes + lax.broadcasted_iota(jnp.int32, shape, 1)
    each = blocks * lanes // 32
    block = ((place.astype(jnp.float32) + jnp.float32(0.5)) * jnp.float32(1.0 / each)).astype(jnp.int32)
    index = found_at(lambda part: order_ref[part : part + 1, :], place + each * (block + core), blocks)
    for at, which in enumerate((0, 1, 2, 4)):
        value = found_at(table(which), index, blocks)
        down[at] = jnp.transpose(value * jnp.float32(turn_scale) if which < 3 else value)


def spread_rows(down_ref, rows_ref, first):
    for which in range(3):
        for block in range(rows_ref.shape[1] // lanes):
            at = first + block
            rows_ref[which, block * lanes : (block + 1) * lanes, :] = jnp.broadcast_to(
                down_ref[which, :, at : at + 1], (lanes, lanes)
            )


def fill_green(rows_ref, columns_ref, tile_ref, first):
    def fill(step, carry):
        rows = pl.ds(pl.multiple_of(step * step_rows, step_rows), step_rows)
        out_rows = pl.ds(pl.multiple_of(first + step * step_rows, step_rows), step_rows)
        row_x, row_y, row_z = [rows_ref[which, rows, :] for which in range(3)]
        for part in range(columns_ref.shape[2] // lanes):
            columns = slice(part * lanes, (part + 1) * lanes)
            col_x, col_y, col_z, col_area = [
                jnp.concatenate([columns_ref[which, :, columns]] * (step_rows // 8), 0) for which in range(4)
            ]
            offset_x, offset_y, offset_z = row_x - col_x, row_y - col_y, row_z - col_z
            square = offset_x * offset_x + offset_y * offset_y
            square = square + (offset_z * offset_z + jnp.float32((smoothing * turn_scale) ** 2))
            inverse = lax.rsqrt(square)
            turns = square * inverse
            half_turn = turns - jnp.round(turns)
            power = half_turn * half_turn
            sine = half_turn * horner(sine_terms, power)
            factor = inverse * col_area
            scaled = sine * factor
            tile_ref[0, out_rows, columns] = (factor - scaled * sine).astype(jnp.bfloat16)
            tile_ref[1, out_rows, columns] = (scaled * horner(cosine_terms, power)).astype(jnp.bfloat16)
        return carry

    lax.fori_loop(0, rows_ref.shape[1] // step_rows, fill, 0)


def first_tile_kernel(
    norm_const,
    order_ref,
    coords_ref,
    areas_ref,
    weights_ref,
    tile_ref,
    columns_ref,
    down_ref,
    halves,
    ids,
    along,
    rows_ref,
):
    place_panels(order_ref, coords_ref, areas_ref, weights_ref, halves, ids, along, down_ref)
    for which in range(4):
        scale = jnp.float32(turn_scale / norm_const if which == 3 else turn_scale)
        for block in range(columns_ref.shape[2] // lanes):
            columns_ref[which, :, block * lanes : (block + 1) * lanes] = jnp.broadcast_to(
                along[which, block : block + 1, :] * scale, (8, lanes)
            )
    spread_rows(down_ref, rows_ref, 0)
    fill_green(rows_ref, columns_ref, tile_ref, 0)


def next_tile_kernel(first, columns_ref, down_ref, filled_ref, tile_ref, rows_ref):
    spread_rows(down_ref, rows_ref, first // lanes)
    fill_green(rows_ref, columns_ref, tile_ref, first)


def tile_cost(row_count, panels):
    pairs = row_count * panels
    return pl.CostEstimate(flops=40 * pairs, bytes_accessed=4 * pairs, transcendentals=3 * pairs)


def first_tile(order, coords, areas, weights, norm_const, row_count):
    blocks = order.shape[0]
    panels = blocks * lanes
    padded = -(-blocks // 8) * 8
    return call(
        functools.partial(first_tile_kernel, norm_const),
        (
            ((2, panels // 2, panels), jnp.bfloat16),
            ((4, 8, panels), jnp.float32),
            ((4, lanes, 8), jnp.float32),
        ),
        (
            ((2, padded, lanes), jnp.int32),
            ((padded, lanes), jnp.int32),
            ((4, padded, lanes), jnp.float32),
            ((3, row_count, lanes), jnp.float32),
        ),
        order,
        coords,
        areas,
        weights,
        cost=tile_cost(row_count, panels),
    )


def next_tile(columns, down, tile, first):
    row_count, panels = tile.shape[1] - first, tile.shape[2]
    return call(
        functools.partial(next_tile_kernel, first),
        ((tile.shape, jnp.bfloat16),),
        (((3, row_count, lanes), jnp.float32),),
        columns,
        down,
        tile,
        cost=tile_cost(row_count, panels),
        aliases={2: 0},
    )[0]


def load_kernel(*refs):
    count = 6
    sources, kept = refs[:count], refs[count : 2 * count - 1]
    terms_ref, sent_ref, velocity, sems = refs[2 * count - 1 :]
    copies = [
        pltpu.make_async_copy(source, target, sems.at[at])
        for at, (source, target) in enumerate(zip(sources, (velocity, *kept)))
    ]
    for copy in copies:
        copy.start()
    copies[0].wait()
    copies[1].wait()
    terms = jnp.dot(kept[0][...], velocity[...], preferred_element_type=jnp.float32)
    terms_ref[...] = terms
    sent_ref[...] = terms.astype(jnp.bfloat16)
    for copy in copies[2:]:
        copy.wait()


def load(modal_velocity, mode_shapes, *tables):
    out = (mode_shapes.shape[0], modal_velocity.shape[1])
    return call(
        load_kernel,
        tuple((value.shape, value.dtype) for value in (mode_shapes, *tables))
        + ((out, jnp.float32), (out, jnp.bfloat16)),
        ((modal_velocity.shape, modal_velocity.dtype), pltpu.SemaphoreType.DMA((6,))),
        *[pltpu.with_memory_space_constraint(value, pltpu.HBM) for value in (modal_velocity, mode_shapes, *tables)],
        specs=[remote] * 6,
    )


def join_kernel(terms_ref, first_ref, second_ref, third_ref, modes_ref, *out_refs):
    chip = lax.axis_index("col") // 2
    count = terms_ref.shape[0]
    total = terms_ref[...]
    for part in (first_ref, second_ref, third_ref):
        total = total + part[...].astype(jnp.float32)
    total = total.astype(jnp.bfloat16)
    for slot, out_ref in enumerate(out_refs):
        out_ref[:count, :] = total
        first = pl.multiple_of((chip ^ slot) * lanes, lanes)
        out_ref[count:, :] = modes_ref[:, pl.ds(first, lanes)]


def turned(value, sign):
    load_count = value.shape[1] // 2
    first, last = value[:, :load_count], value[:, load_count:]
    if sign > 0:
        return jnp.concatenate([-last, first], 1)
    return jnp.concatenate([last, -first], 1)


def tile_dot(tile_ref, columns, value, sign):
    return jnp.dot(
        tile_ref[0, :, columns], value, preferred_element_type=jnp.float32
    ) + jnp.dot(tile_ref[1, :, columns], turned(value, sign), preferred_element_type=jnp.float32)


def own_pressure_kernel(tile_ref, value_ref, down_ref, out_ref, weight_ref):
    out_ref[...] = tile_dot(tile_ref, slice(0, value_ref.shape[0]), value_ref[...], 1)
    for block in range(weight_ref.shape[0] // lanes):
        weight_ref[block * lanes : (block + 1) * lanes, :] = jnp.broadcast_to(
            down_ref[3, :, block : block + 1], (lanes, lanes)
        )


def other_pressure_kernel(tile_ref, value_ref, term_ref, out_ref):
    half = value_ref.shape[0]
    out_ref[...] = term_ref[...] + tile_dot(tile_ref, slice(half, 2 * half), value_ref[...], 1)


def modal_kernel(tile_ref, value_ref, weight_ref, own_ref, other_ref, *refs):
    kept_ref, sent_ref = refs
    col = lax.axis_index("col")
    source = (value_ref[...] * weight_ref[...]).astype(jnp.bfloat16)
    sensitivity = sum(
        jnp.dot(jnp.transpose(value), tile_ref[part], preferred_element_type=jnp.float32)
        for part, value in enumerate((source, turned(source, -1)))
    ).astype(jnp.bfloat16)
    half = own_ref.shape[0]
    modal = jnp.dot(sensitivity[:, :half], own_ref[...], preferred_element_type=jnp.float32)
    modal = modal + jnp.dot(sensitivity[:, half:], other_ref[...], preferred_element_type=jnp.float32)
    modal = jnp.transpose(modal)
    modes_each = kept_ref.shape[0]
    low, high = modal[:modes_each, :], modal[modes_each:, :]
    kept_ref[...] = jnp.where(col % 2 == 0, low, high)
    sent_ref[...] = jnp.where(col % 2 == 0, high, low)


def own_rows_kernel(value_ref, out_ref):
    each = out_ref.shape[0]
    block = (lax.axis_index("row") * lax.axis_size("col") + lax.axis_index("col")) // 2
    out_ref[...] = value_ref[pl.ds(pl.multiple_of(block * each, each), each), :]


def swap(value, axis, mask):
    return lax.ppermute(value, axis, [(i, i ^ mask) for i in range(lax.axis_size(axis))])


def local(modal_velocity, mode_shapes, coords, panel_order, areas, weights):
    panels = panel_order.shape[0]
    norm_const = math.sqrt(4.0 * math.pi * panels)
    own_rows, load_columns = mode_shapes.shape[0], modal_velocity.shape[1]
    half = 4 * own_rows
    part_rows = half // 2
    wide = (panels // lanes, lanes)
    modes, order, coords, areas, weights, terms, sent = load(
        modal_velocity,
        mode_shapes,
        panel_order.reshape(wide),
        coords,
        areas.reshape(wide),
        weights.reshape(wide),
    )
    received = [swap(sent, "row", mask) for mask in (1, 2, 3)]
    tiles = first_tile(order, coords, areas, weights, norm_const, part_rows)
    received, tiles = lax.optimization_barrier((received, tiles))
    tile, columns, down = tiles
    joined = call(
        join_kernel, (((2 * own_rows, load_columns), jnp.bfloat16),) * 4, (), terms, *received, modes
    )
    received = [swap(value, "col", 2 * mask) for mask, value in zip((3, 2, 1), joined[:0:-1])]
    tile = next_tile(columns, down, tile, part_rows)
    received, tile = lax.optimization_barrier((received, tile))
    joined = [joined[0], *received[::-1]]
    own = jnp.concatenate([value[:own_rows] for value in joined], 0)
    modes = jnp.concatenate([value[own_rows:] for value in joined], 0)
    other = swap(own, "col", 1)
    other_modes = swap(modes, "col", 1)
    out = ((half, load_columns), jnp.float32)
    term, weight = call(
        own_pressure_kernel, (out, ((half, lanes), jnp.float32)), (), tile, own, down
    )
    pressure = call(other_pressure_kernel, (out,), (), tile, other, term)[0]
    modes_each = mode_shapes.shape[1] // 8
    kept, sent = call(
        modal_kernel,
        (((modes_each, load_columns), jnp.float32),) * 2,
        (),
        tile,
        pressure,
        weight,
        modes,
        other_modes,
    )
    each = own_rows // lax.axis_size("row")
    own_pressure = call(own_rows_kernel, (((each, load_columns), jnp.float32),), (), pressure)[0]
    return (own_pressure, kept + swap(sent, "col", 1))


def solution(mesh):
    in_specs = (P("row", None), P("col", "row"), P(), P(), P(), P())
    out_specs = (P(("row", "col"), None), P(("row", "col"), None))

    def body(*args):
        panels = args[3].shape[0]
        small = mesh.shape["row"] == 4 and mesh.shape["col"] == 8 and panels == 1536
        return (local if small else local_general)(*args)

    return jax.shard_map(body, mesh=mesh, in_specs=in_specs, out_specs=out_specs, check_vma=False)
```

```python
import functools
import math

import jax
import jax.numpy as jnp
from jax import lax
from jax.experimental import pallas as pl
from jax.experimental.pallas import tpu as pltpu
from jax.sharding import PartitionSpec as P

wavenumber = 20.0
smoothing = 0.02


def green_rows(target, source, source_area, norm_const):
    offset = target[0][:, None] - source[0][None, :]
    square = offset * offset
    offset = target[1][:, None] - source[1][None, :]
    square = square + offset * offset
    offset = target[2][:, None] - source[2][None, :]
    square = square + offset * offset
    distance = jnp.sqrt(square + smoothing * smoothing)
    factor = source_area[None, :] / (distance * norm_const)
    angle_value = wavenumber * distance
    return jnp.stack([factor * jnp.cos(angle_value), factor * jnp.sin(angle_value)]).astype(
        jnp.bfloat16
    )


def make_tile(target, source, source_area, norm_const):
    row_count = target.shape[1]
    if row_count <= 1024 or row_count % 512 != 0:
        return green_rows(target, source, source_area, norm_const)
    buffer = jnp.zeros((2, row_count, source.shape[1]), jnp.bfloat16)

    def fill(block_index, current):
        first_row = block_index * 512
        target_part = lax.dynamic_slice_in_dim(target, first_row, 512, 1)
        return lax.dynamic_update_slice_in_dim(
            current, green_rows(target_part, source, source_area, norm_const), first_row, 1
        )

    return lax.fori_loop(0, row_count // 512, fill, buffer)


def forward_parts(products, load_count):
    real_part = products[0, :, :load_count] - products[1, :, load_count:]
    imag_part = products[0, :, load_count:] + products[1, :, :load_count]
    return jnp.concatenate([real_part, imag_part], axis=1)


def adjoint_parts(products, load_count):
    real_part = products[0, :, :load_count] + products[1, :, load_count:]
    imag_part = products[0, :, load_count:] - products[1, :, :load_count]
    return jnp.concatenate([real_part, imag_part], axis=1)


def row_total(partial_value):
    return lax.psum(partial_value, "row").astype(jnp.bfloat16)


def local_general(modal_velocity, mode_shapes, coords, panel_order, areas, weights):
    row_index = lax.axis_index("row")
    col_index = lax.axis_index("col")
    src_rows = mode_shapes.shape[0]
    panels_each = src_rows // lax.axis_size("row")
    tgt_rows = panels_each * lax.axis_size("col")
    panel_total = panel_order.shape[0]
    norm_const = math.sqrt(4.0 * math.pi * panel_total)
    load_count = modal_velocity.shape[1] // 2
    target_ids = lax.dynamic_slice_in_dim(panel_order, row_index * tgt_rows, tgt_rows)
    source_ids = lax.dynamic_slice_in_dim(panel_order, col_index * src_rows, src_rows)
    target_xyz = jnp.take(coords, target_ids, axis=1)
    source_xyz = jnp.take(coords, source_ids, axis=1)
    source_area = jnp.take(areas, source_ids)
    target_weight = jnp.take(weights, target_ids)
    stored = make_tile(target_xyz, source_xyz, source_area, norm_const)

    def tile_rows():
        return stored

    surface = row_total(jnp.dot(mode_shapes, modal_velocity, preferred_element_type=jnp.float32))
    products = jnp.einsum("krm,mc->krc", tile_rows(), surface, preferred_element_type=jnp.float32)
    pressure = lax.psum_scatter(
        forward_parts(products, load_count), "col", scatter_dimension=0, tiled=True
    )
    own_weight = lax.dynamic_slice_in_dim(target_weight, col_index * panels_each, panels_each)
    source_terms = (pressure * own_weight[:, None]).astype(jnp.bfloat16)
    products = jnp.einsum(
        "krm,rc->kmc",
        tile_rows(),
        lax.all_gather(source_terms, "col", axis=0, tiled=True),
        preferred_element_type=jnp.float32,
    )
    sensitivity = adjoint_parts(products, load_count)
    summed = row_total(sensitivity)
    modal_terms = lax.dot_general(
        mode_shapes, summed, (((0,), (0,)), ((), ())), preferred_element_type=jnp.float32
    )
    gradient = lax.psum_scatter(modal_terms, "col", scatter_dimension=0, tiled=True)
    return (pressure, gradient)


sine_terms = (4.442879676818848, -7.307816505432129, 3.5977742671966553, -0.7911993861198425)
cosine_terms = (1.4142040014266968, -6.97763729095459, 5.715188026428223, -1.728213906288147)
turn_scale = wavenumber / (2.0 * math.pi)
lanes = 128
step_rows = 64
whole = pl.BlockSpec(memory_space=pltpu.VMEM)
remote = pl.BlockSpec(memory_space=pltpu.HBM)


def call(kernel, shapes, scratch, *args, cost=None, specs=None, outs=None, aliases=None):
    shapes = tuple(jax.ShapeDtypeStruct(shape, dtype) for shape, dtype in shapes)
    return pl.pallas_call(
        kernel,
        out_shape=shapes,
        in_specs=specs or [whole] * len(args),
        out_specs=outs or (whole,) * len(shapes),
        scratch_shapes=[pltpu.VMEM(*entry) if isinstance(entry, tuple) else entry for entry in scratch],
        compiler_params=pltpu.CompilerParams(vmem_limit_bytes=16 * 2**20),
        cost_estimate=cost,
        input_output_aliases=aliases or {},
    )(*args)


def horner(terms, value):
    total = jnp.float32(terms[-1])
    for term in terms[-2::-1]:
        total = jnp.float32(term) + value * total
    return total


def found_at(row_of, index, count):
    high, low = index // lanes, index % lanes
    total = None
    for part in range(count):
        row = row_of(part)
        found = jnp.take_along_axis(
            jnp.broadcast_to(row, index.shape), low, axis=1, mode="promise_in_bounds"
        )
        total = jnp.where(high == part, found, jnp.zeros_like(found) if total is None else total)
    return total


def place_panels(order_ref, coords_ref, areas_ref, weights_ref, halves, ids, along, down):
    col = lax.axis_index("col")
    chip, core = col // 2, col % 2
    blocks = order_ref.shape[0]
    first_half = lax.broadcasted_iota(jnp.int32, (1, lanes), 1) < lanes // 2
    halves[0, :blocks, :] = order_ref[...]
    halves[1, :blocks, :] = pltpu.roll(order_ref[...], lanes // 2, 1)
    ids[...] = jnp.zeros(ids.shape, jnp.int32)
    for block in range(blocks):
        found = []
        for at in (2 * block, 2 * block + 1):
            side, slot, part = at // blocks, at % blocks // 3, at % 3
            panel_block = 2 * (chip ^ slot) + (core if side == 0 else 1 - core)
            source = 3 * panel_block + part
            found.append(halves[(source + at) % 2, pl.ds(source // 2, 1), :])
        ids[block : block + 1, :] = jnp.where(first_half, found[0], found[1])

    def table(which):
        if which < 3:
            return lambda part: coords_ref[which : which + 1, part * lanes : (part + 1) * lanes]
        source = areas_ref if which == 3 else weights_ref
        return lambda part: source[part : part + 1, :]

    for group in range(ids.shape[0] // 8):
        rows = slice(8 * group, 8 * group + 8)
        for which in range(4):
            along[which, rows, :] = found_at(table(which), ids[rows, :], blocks)
    shape = (8, lanes)
    place = lax.broadcasted_iota(jnp.int32, shape, 0) * lanes + lax.broadcasted_iota(jnp.int32, shape, 1)
    each = blocks * lanes // 32
    block = ((place.astype(jnp.float32) + jnp.float32(0.5)) * jnp.float32(1.0 / each)).astype(jnp.int32)
    index = found_at(lambda part: order_ref[part : part + 1, :], place + each * (block + core), blocks)
    for at, which in enumerate((0, 1, 2, 4)):
        value = found_at(table(which), index, blocks)
        down[at] = jnp.transpose(value * jnp.float32(turn_scale) if which < 3 else value)


def spread_rows(down_ref, rows_ref, first):
    for which in range(3):
        for block in range(rows_ref.shape[1] // lanes):
            at = first + block
            rows_ref[which, block * lanes : (block + 1) * lanes, :] = jnp.broadcast_to(
                down_ref[which, :, at : at + 1], (lanes, lanes)
            )


def fill_green(rows_ref, columns_ref, tile_ref, first):
    def fill(step, carry):
        rows = pl.ds(pl.multiple_of(step * step_rows, step_rows), step_rows)
        out_rows = pl.ds(pl.multiple_of(first + step * step_rows, step_rows), step_rows)
        row_x, row_y, row_z = [rows_ref[which, rows, :] for which in range(3)]
        for part in range(columns_ref.shape[2] // lanes):
            columns = slice(part * lanes, (part + 1) * lanes)
            col_x, col_y, col_z, col_area = [
                jnp.concatenate([columns_ref[which, :, columns]] * (step_rows // 8), 0) for which in range(4)
            ]
            offset_x, offset_y, offset_z = row_x - col_x, row_y - col_y, row_z - col_z
            square = offset_x * offset_x + offset_y * offset_y
            square = square + (offset_z * offset_z + jnp.float32((smoothing * turn_scale) ** 2))
            inverse = lax.rsqrt(square)
            turns = square * inverse
            half_turn = turns - jnp.round(turns)
            power = half_turn * half_turn
            sine = half_turn * horner(sine_terms, power)
            factor = inverse * col_area
            scaled = sine * factor
            tile_ref[0, out_rows, columns] = (factor - scaled * sine).astype(jnp.bfloat16)
            tile_ref[1, out_rows, columns] = (scaled * horner(cosine_terms, power)).astype(jnp.bfloat16)
        return carry

    lax.fori_loop(0, rows_ref.shape[1] // step_rows, fill, 0)


def first_tile_kernel(
    norm_const,
    order_ref,
    coords_ref,
    areas_ref,
    weights_ref,
    tile_ref,
    columns_ref,
    down_ref,
    halves,
    ids,
    along,
    rows_ref,
):
    place_panels(order_ref, coords_ref, areas_ref, weights_ref, halves, ids, along, down_ref)
    for which in range(4):
        scale = jnp.float32(turn_scale / norm_const if which == 3 else turn_scale)
        for block in range(columns_ref.shape[2] // lanes):
            columns_ref[which, :, block * lanes : (block + 1) * lanes] = jnp.broadcast_to(
                along[which, block : block + 1, :] * scale, (8, lanes)
            )
    spread_rows(down_ref, rows_ref, 0)
    fill_green(rows_ref, columns_ref, tile_ref, 0)


def next_tile_kernel(first, columns_ref, down_ref, filled_ref, tile_ref, rows_ref):
    spread_rows(down_ref, rows_ref, first // lanes)
    fill_green(rows_ref, columns_ref, tile_ref, first)


def tile_cost(row_count, panels):
    pairs = row_count * panels
    return pl.CostEstimate(flops=40 * pairs, bytes_accessed=4 * pairs, transcendentals=3 * pairs)


def first_tile(order, coords, areas, weights, norm_const, row_count):
    blocks = order.shape[0]
    panels = blocks * lanes
    padded = -(-blocks // 8) * 8
    return call(
        functools.partial(first_tile_kernel, norm_const),
        (
            ((2, panels // 2, panels), jnp.bfloat16),
            ((4, 8, panels), jnp.float32),
            ((4, lanes, 8), jnp.float32),
        ),
        (
            ((2, padded, lanes), jnp.int32),
            ((padded, lanes), jnp.int32),
            ((4, padded, lanes), jnp.float32),
            ((3, row_count, lanes), jnp.float32),
        ),
        order,
        coords,
        areas,
        weights,
        cost=tile_cost(row_count, panels),
    )


def next_tile(columns, down, tile, first):
    row_count, panels = tile.shape[1] - first, tile.shape[2]
    return call(
        functools.partial(next_tile_kernel, first),
        ((tile.shape, jnp.bfloat16),),
        (((3, row_count, lanes), jnp.float32),),
        columns,
        down,
        tile,
        cost=tile_cost(row_count, panels),
        aliases={2: 0},
    )[0]


def load_kernel(*refs):
    count = 6
    sources, kept = refs[:count], refs[count : 2 * count - 1]
    terms_ref, sent_ref, velocity, sems = refs[2 * count - 1 :]
    copies = [
        pltpu.make_async_copy(source, target, sems.at[at])
        for at, (source, target) in enumerate(zip(sources, (velocity, *kept)))
    ]
    for copy in copies:
        copy.start()
    copies[0].wait()
    copies[1].wait()
    terms = jnp.dot(kept[0][...], velocity[...], preferred_element_type=jnp.float32)
    terms_ref[...] = terms
    sent_ref[...] = terms.astype(jnp.bfloat16)
    for copy in copies[2:]:
        copy.wait()


def load(modal_velocity, mode_shapes, *tables):
    out = (mode_shapes.shape[0], modal_velocity.shape[1])
    return call(
        load_kernel,
        tuple((value.shape, value.dtype) for value in (mode_shapes, *tables))
        + ((out, jnp.float32), (out, jnp.bfloat16)),
        ((modal_velocity.shape, modal_velocity.dtype), pltpu.SemaphoreType.DMA((6,))),
        *[pltpu.with_memory_space_constraint(value, pltpu.HBM) for value in (modal_velocity, mode_shapes, *tables)],
        specs=[remote] * 6,
    )


def join_kernel(terms_ref, first_ref, second_ref, third_ref, modes_ref, *out_refs):
    chip = lax.axis_index("col") // 2
    count = terms_ref.shape[0]
    total = terms_ref[...]
    for part in (first_ref, second_ref, third_ref):
        total = total + part[...].astype(jnp.float32)
    total = total.astype(jnp.bfloat16)
    for slot, out_ref in enumerate(out_refs):
        out_ref[:count, :] = total
        first = pl.multiple_of((chip ^ slot) * lanes, lanes)
        out_ref[count:, :] = modes_ref[:, pl.ds(first, lanes)]


def turned(value, sign):
    load_count = value.shape[1] // 2
    first, last = value[:, :load_count], value[:, load_count:]
    if sign > 0:
        return jnp.concatenate([-last, first], 1)
    return jnp.concatenate([last, -first], 1)


def tile_dot(tile_ref, columns, value, sign):
    return jnp.dot(
        tile_ref[0, :, columns], value, preferred_element_type=jnp.float32
    ) + jnp.dot(tile_ref[1, :, columns], turned(value, sign), preferred_element_type=jnp.float32)


def own_pressure_kernel(tile_ref, value_ref, down_ref, out_ref, weight_ref):
    out_ref[...] = tile_dot(tile_ref, slice(0, value_ref.shape[0]), value_ref[...], 1)
    for block in range(weight_ref.shape[0] // lanes):
        weight_ref[block * lanes : (block + 1) * lanes, :] = jnp.broadcast_to(
            down_ref[3, :, block : block + 1], (lanes, lanes)
        )


def other_pressure_kernel(tile_ref, value_ref, term_ref, out_ref):
    half = value_ref.shape[0]
    out_ref[...] = term_ref[...] + tile_dot(tile_ref, slice(half, 2 * half), value_ref[...], 1)


def modal_kernel(tile_ref, value_ref, weight_ref, own_ref, other_ref, *refs):
    kept_ref, sent_ref = refs
    col = lax.axis_index("col")
    source = (value_ref[...] * weight_ref[...]).astype(jnp.bfloat16)
    sensitivity = sum(
        jnp.dot(jnp.transpose(value), tile_ref[part], preferred_element_type=jnp.float32)
        for part, value in enumerate((source, turned(source, -1)))
    ).astype(jnp.bfloat16)
    half = own_ref.shape[0]
    modal = jnp.dot(sensitivity[:, :half], own_ref[...], preferred_element_type=jnp.float32)
    modal = modal + jnp.dot(sensitivity[:, half:], other_ref[...], preferred_element_type=jnp.float32)
    modal = jnp.transpose(modal)
    modes_each = kept_ref.shape[0]
    low, high = modal[:modes_each, :], modal[modes_each:, :]
    kept_ref[...] = jnp.where(col % 2 == 0, low, high)
    sent_ref[...] = jnp.where(col % 2 == 0, high, low)


def own_rows_kernel(value_ref, out_ref):
    each = out_ref.shape[0]
    block = (lax.axis_index("row") * lax.axis_size("col") + lax.axis_index("col")) // 2
    out_ref[...] = value_ref[pl.ds(pl.multiple_of(block * each, each), each), :]


def swap(value, axis, mask):
    return lax.ppermute(value, axis, [(i, i ^ mask) for i in range(lax.axis_size(axis))])


def local(modal_velocity, mode_shapes, coords, panel_order, areas, weights):
    panels = panel_order.shape[0]
    norm_const = math.sqrt(4.0 * math.pi * panels)
    own_rows, load_columns = mode_shapes.shape[0], modal_velocity.shape[1]
    half = 4 * own_rows
    part_rows = half // 2
    wide = (panels // lanes, lanes)
    modes, order, coords, areas, weights, terms, sent = load(
        modal_velocity,
        mode_shapes,
        panel_order.reshape(wide),
        coords,
        areas.reshape(wide),
        weights.reshape(wide),
    )
    received = [swap(sent, "row", mask) for mask in (1, 3, 2)]
    tiles = first_tile(order, coords, areas, weights, norm_const, part_rows)
    received, tiles = lax.optimization_barrier((received, tiles))
    tile, columns, down = tiles
    joined = call(
        join_kernel, (((2 * own_rows, load_columns), jnp.bfloat16),) * 4, (), terms, *received, modes
    )
    received = [swap(value, "col", 2 * mask) for mask, value in zip((3, 1, 2), (joined[3], joined[1], joined[2]))]
    tile = next_tile(columns, down, tile, part_rows)
    received, tile = lax.optimization_barrier((received, tile))
    joined = [joined[0], received[1], received[2], received[0]]
    own = jnp.concatenate([value[:own_rows] for value in joined], 0)
    modes = jnp.concatenate([value[own_rows:] for value in joined], 0)
    other = swap(own, "col", 1)
    other_modes = swap(modes, "col", 1)
    out = ((half, load_columns), jnp.float32)
    term, weight = call(
        own_pressure_kernel, (out, ((half, lanes), jnp.float32)), (), tile, own, down
    )
    pressure = call(other_pressure_kernel, (out,), (), tile, other, term)[0]
    modes_each = mode_shapes.shape[1] // 8
    kept, sent = call(
        modal_kernel,
        (((modes_each, load_columns), jnp.float32),) * 2,
        (),
        tile,
        pressure,
        weight,
        modes,
        other_modes,
    )
    each = own_rows // lax.axis_size("row")
    own_pressure = call(own_rows_kernel, (((each, load_columns), jnp.float32),), (), pressure)[0]
    return (own_pressure, kept + swap(sent, "col", 1))


def solution(mesh):
    in_specs = (P("row", None), P("col", "row"), P(), P(), P(), P())
    out_specs = (P(("row", "col"), None), P(("row", "col"), None))

    def body(*args):
        panels = args[3].shape[0]
        small = mesh.shape["row"] == 4 and mesh.shape["col"] == 8 and panels == 1536
        return (local if small else local_general)(*args)

    return jax.shard_map(body, mesh=mesh, in_specs=in_specs, out_specs=out_specs, check_vma=False)
```
